128 devices in a mesh: dp: 4 (over y), expert: 32 (over x, z, core).
Axes of the slice: x: 4, y: 4, z: 4, core: 2. Of those that a mesh axis runs over, the one named last changes fastest.
Arguments:
- tokens: bfloat16 [4096, 2048], P('expert', 'dp'), may hold values from -6 to 6
- picks: int32 [2, 4096, 16], P(None, 'expert'), may hold values from 0 to 255, all different within a row; in each aligned block of 128 rows (0 to 127, 128 to 255, ..., all dimensions but the last counted through in order) at most 10 rows name the same one
- halting: int32 [4096], P('expert'), may hold values from 1 to 2
- w_sel: bfloat16 [2048, 256], P('dp'), may hold values from -0.125 to 0.125
- w_up: bfloat16 [256, 2048, 256], P('expert', 'dp'), may hold values from -0.125 to 0.125
- w_down: bfloat16 [256, 256, 2048], P('expert', None, 'dp'), may hold values from -0.1875 to 0.1875
- cotangent: bfloat16 [4096, 2048], P('expert', 'dp'), may hold values from -6 to 6
Outputs:
- layer_out: bfloat16 [4096, 2048], P('expert', 'dp')
- d_tokens: bfloat16 [4096, 2048], P('expert', 'dp')
- d_up: float32 [256, 2048, 256], P('expert', 'dp')
- d_down: float32 [256, 256, 2048], P('expert', None, 'dp')
- d_sel: float32 [2048, 256], P('dp')
The draws below stay inside these ranges and needn't reach their ends.
Inputs may be any that keep to these rules, and one draw needn't show every extreme that they name: `picks`: each row names 16 different experts. In each pass the 128 tokens of one device name any one expert at most 10 times, a bound that some block reaches. `halting`: the number of passes a token takes.
All inputs are finite; a program needn't handle non-finite values.
Results may differ from the reference program's by a relative error of at most 0.034.
Values may be sent and summed in bfloat16 or wider, within the bound.
No kernel may reach another device: no remote copies, remote signals or barrier semaphores. Data moves between devices by JAX's collectives and lax.ppermute only.
A program may use at most 128 MiB of HBM per device.

```python
import math
import jax
import jax.numpy as jnp
import numpy as np
from jax import lax

D = 2048
H = 256
TOPK = 16
PASSES = 2
TOK_DEV = 128
EXPERTS = 256
TOKENS = 4096
CAP = 10
N_DP = 4
N_EXPERT = 32


def plant(values, rng, least, largest):
    extent = values.shape
    place = [jax.random.randint(jax.random.fold_in(rng, axis), (), 0, extent[axis]) for axis in range(len(extent))]
    values = values.at[tuple(place)].set(least)
    longest = extent.index(max(extent))
    place[longest] = (place[longest] + 1) % extent[longest]
    return values.at[tuple(place)].set(largest)


def steps_of(own_key, dims, cuts, smallest, high):
    gain = 1.0
    for position, shards_of in cuts:
        steps = jax.random.uniform(jax.random.fold_in(jax.random.fold_in(own_key, 6), position), (shards_of,), jnp.float32, smallest / len(cuts), high / len(cuts))
        gain = gain * jnp.repeat(jnp.exp(steps), dims[position] // shards_of).reshape((-1,) + (1,) * (len(dims) - 1 - position))
    return gain


def routed_block(key, own, number, rows, amount, top, reach, lean):
    sequence = jax.random.permutation(key, amount)
    crowded, usual = portions_of(amount, rows * top, reach, lean, True), portions_of(amount, rows * top, reach, lean, False)
    places = jnp.arange(amount)

    def named(lengths, offset_by):
        used = int((lengths > 0).sum())
        fixed = max(1, used // 4)
        shifted = fixed + (places - fixed + offset_by * (used - fixed)) % max(1, amount - fixed)
        return jnp.zeros((amount,), jnp.int32).at[sequence[jnp.where(places < fixed, places, shifted)]].set(jnp.asarray(lengths, jnp.int32))

    lengths = jnp.where(number % 4 == 0, named(crowded, number // 4), named(usual, number - number // 4 - 1))
    mixed = jax.random.permutation(jax.random.fold_in(own, 3), amount)
    donor, sink = mixed[0:amount // 2 * 2:2], mixed[1:amount // 2 * 2:2]
    room = jnp.minimum(lengths[donor] - 1, reach - lengths[sink]) // 2
    room = jnp.where((donor == sequence[0]) | (sink == sequence[0]) | (lengths[sink] == 0), 0, jnp.maximum(room, 0))
    shifted = jax.random.randint(jax.random.fold_in(own, 4), (amount // 2,), 0, 1 << 20) % (room + 1)
    lengths = lengths.at[donor].add(-shifted).at[sink].add(shifted)
    members = jnp.searchsorted(jnp.cumsum(lengths), jnp.arange(rows * top), side="right").astype(jnp.int32)
    grid = members.reshape(top, rows).T
    grid = grid[jax.random.permutation(jax.random.fold_in(own, 1), rows)]
    offset_by = jax.random.randint(jax.random.fold_in(own, 2), (rows, 1), 0, top)
    return jnp.take_along_axis(grid, (jnp.arange(top)[None, :] + offset_by) % top, axis=1)


def portions_of(number_of, total, reach, lean, full):
    portions = [(1 << 20) // math.isqrt(standing ** lean) + 1 for standing in range(1, number_of + 1)]
    largest = reach if full else min(reach, max(-(-total // number_of), total * portions[0] // sum(portions)))
    least = 1 if total - largest >= number_of - 1 else 0
    given, rest = [largest] + [least] * (number_of - 1), total - largest - least * (number_of - 1)
    while rest > 0:
        movable = [i for i in range(1, number_of) if given[i] < largest] or [i for i in range(1, number_of) if given[i] < reach]
        whole, budget = sum([portions[i] for i in movable]), rest
        for i in movable:
            more = min(reach - given[i], max(1, budget * portions[i] // whole), rest)
            given[i] = given[i] + more
            rest = rest - more
    return np.array(given)


def centred(key, dims, width, bound, cuts=(), held_as=jnp.bfloat16):
    drawn = width * jax.random.normal(key, dims, jnp.float32)
    if cuts:
        drawn = drawn * steps_of(key, dims, cuts, -0.22, 0.18)
    return jnp.clip(drawn, -bound, bound).astype(held_as)


def setup_inputs(seed: int = 0) -> dict:
    streams_of = jax.random.split(jax.random.key(seed), 8)
    tokens = centred(streams_of[0], (TOKENS, D), 1.0, 6.0, ((0, 32), (1, 4)))
    picks_keys = jax.random.split(jax.random.fold_in(streams_of[1], 1), PASSES * TOKENS // TOK_DEV)
    picks_turns = jax.random.permutation(jax.random.fold_in(streams_of[1], 3), PASSES * TOKENS // TOK_DEV)
    picks = jax.vmap(lambda own, number: routed_block(jax.random.fold_in(streams_of[1], 2), own, number, TOK_DEV, EXPERTS, TOPK, CAP, 2))(picks_keys, picks_turns).reshape((PASSES, TOKENS, TOPK))
    halting = plant(jax.random.randint(streams_of[2], (TOKENS,), 1, 3), jax.random.fold_in(streams_of[2], 1), 1, 2).astype(jnp.int32)
    w_sel = centred(streams_of[3], (D, EXPERTS), D ** -0.5, 0.125, ((0, 4),))
    w_up = centred(streams_of[4], (EXPERTS, D, H), D ** -0.5, 0.125, ((0, 32), (1, 4)))
    w_down = centred(streams_of[5], (EXPERTS, H, D), (H * 4) ** -0.5, 0.1875, ((0, 32), (2, 4)))
    cotangent = centred(streams_of[6], (TOKENS, D), 1.0, 6.0, ((0, 32), (1, 4)))
    return {"tokens": tokens, "picks": picks, "halting": halting, "w_sel": w_sel, "w_up": w_up, "w_down": w_down, "cotangent": cotangent}


GELU_C = 0.7978845608028654
GELU_A = 0.044715


def gelu_tanh(pre_act):
    inner = GELU_C * (pre_act + GELU_A * pre_act * pre_act * pre_act)
    return 0.5 * pre_act * (1.0 + jnp.tanh(inner))


def gelu_slope(pre_act):
    inner = GELU_C * (pre_act + GELU_A * pre_act * pre_act * pre_act)
    tangent = jnp.tanh(inner)
    return 0.5 * (1.0 + tangent) + 0.5 * pre_act * (1.0 - tangent * tangent) * GELU_C * (1.0 + 3.0 * GELU_A * pre_act * pre_act)


def partial_total(partials):
    rounded = lax.optimization_barrier(partials.astype(jnp.bfloat16))
    return jnp.sum(rounded.astype(jnp.float32), axis=0)


def routing(chosen):
    flat_ids = chosen.reshape(-1).astype(jnp.int32)
    sort_order = jnp.argsort(flat_ids, stable=True).astype(jnp.int32)
    expert_ids = jnp.arange(EXPERTS, dtype=jnp.int32)
    counts = jnp.sum((flat_ids[:, None] == expert_ids[None, :]).astype(jnp.int32), axis=0)
    starts = (jnp.cumsum(counts) - counts).astype(jnp.int32)
    return sort_order, starts, counts


def expert_slots(sort_order, starts, counts, expert):
    span_rows = N_EXPERT * CAP
    offsets = jnp.arange(span_rows, dtype=jnp.int32)
    where_at = jnp.clip(starts[expert] + offsets, 0, sort_order.shape[0] - 1).astype(jnp.int32)
    pick_ids = sort_order[where_at]
    usable = offsets < counts[expert]
    return pick_ids, usable


def expert_forward(row_block, up_mat, down_mat):
    total_rows = row_block.shape[0]
    pieces = row_block.astype(jnp.float32).reshape(total_rows, N_DP, -1)
    up_pieces = up_mat.astype(jnp.float32).reshape(N_DP, -1, up_mat.shape[1])
    partials = jnp.einsum('rjd,jdh->jrh', pieces, up_pieces)
    pre_act = partial_total(partials)
    hidden = gelu_tanh(pre_act).astype(jnp.bfloat16)
    outputs = jnp.dot(hidden, down_mat, preferred_element_type=jnp.float32).astype(jnp.bfloat16)
    return pre_act, hidden, outputs


def expert_backward(row_block, pre_act, hidden, grad_out, up_mat, down_mat):
    total_rows = row_block.shape[0]
    pieces = grad_out.astype(jnp.float32).reshape(total_rows, N_DP, -1)
    down_pieces = down_mat.astype(jnp.float32).reshape(down_mat.shape[0], N_DP, -1)
    partials = jnp.einsum('rjd,hjd->jrh', pieces, down_pieces)
    grad_hidden = partial_total(partials)
    grad_pre = (grad_hidden * gelu_slope(pre_act)).astype(jnp.bfloat16)
    grad_rows = jnp.dot(grad_pre, up_mat.T, preferred_element_type=jnp.float32).astype(jnp.bfloat16)
    grad_down = jnp.dot(hidden.T, grad_out, preferred_element_type=jnp.float32)
    grad_up = jnp.dot(row_block.T, grad_pre, preferred_element_type=jnp.float32)
    return grad_rows, grad_down, grad_up


def forward_pass(current, chosen, weights_tk, w_up, w_down):
    sort_order, starts, counts = routing(chosen)
    flat_weight = weights_tk.reshape(-1)

    def per_expert(running, expert):
        pick_ids, usable = expert_slots(sort_order, starts, counts, expert)
        token_ids = pick_ids // TOPK
        row_block = jnp.where(usable[:, None], current[token_ids], jnp.zeros((), jnp.bfloat16))
        pre_act, hidden, outputs = expert_forward(row_block, w_up[expert], w_down[expert])
        row_weight = jnp.where(usable, flat_weight[pick_ids], jnp.float32(0.0))
        running = running.at[token_ids].add(row_weight[:, None] * outputs.astype(jnp.float32))
        return running, None

    mixed_sum, unused_out = lax.scan(per_expert, jnp.zeros(current.shape, jnp.float32), jnp.arange(EXPERTS, dtype=jnp.int32))
    return (current.astype(jnp.float32) + mixed_sum).astype(jnp.bfloat16)


def backward_pass(current, chosen, weights_tk, active, gate_prob, cot_now, w_up, w_down, w_sel):
    sort_order, starts, counts = routing(chosen)
    flat_weight = weights_tk.reshape(-1)
    cot_wide = cot_now.astype(jnp.float32)

    def per_expert(running, expert):
        grad_state, score_grad = running
        pick_ids, usable = expert_slots(sort_order, starts, counts, expert)
        token_ids = pick_ids // TOPK
        row_block = jnp.where(usable[:, None], current[token_ids], jnp.zeros((), jnp.bfloat16))
        pre_act, hidden, outputs = expert_forward(row_block, w_up[expert], w_down[expert])
        cot_rows = cot_wide[token_ids]
        row_weight = jnp.where(usable, flat_weight[pick_ids], jnp.float32(0.0))
        grad_out = (row_weight[:, None] * cot_rows).astype(jnp.bfloat16)
        dot_terms = jnp.sum(cot_rows * outputs.astype(jnp.float32), axis=1) * active[token_ids]
        score_grad = score_grad.at[pick_ids].add(jnp.where(usable, dot_terms, jnp.float32(0.0)))
        grad_rows, grad_down, grad_up = expert_backward(row_block, pre_act, hidden, grad_out, w_up[expert], w_down[expert])
        grad_state = grad_state.at[token_ids].add(jnp.where(usable[:, None], grad_rows.astype(jnp.float32), jnp.float32(0.0)))
        return (grad_state, score_grad), (grad_up, grad_down)

    start_carry = (jnp.zeros(current.shape, jnp.float32), jnp.zeros((chosen.shape[0] * TOPK,), jnp.float32))
    (grad_state, score_grad), (grads_up, grads_down) = lax.scan(per_expert, start_carry, jnp.arange(EXPERTS, dtype=jnp.int32))
    score_grad = score_grad.reshape(chosen.shape)
    logit_grad = score_grad * gate_prob * (1.0 - gate_prob)
    expert_ids = jnp.arange(EXPERTS, dtype=jnp.int32)
    pick_table = jnp.sum(logit_grad[:, :, None] * (chosen[:, :, None] == expert_ids[None, None, :]).astype(jnp.float32), axis=1).astype(jnp.bfloat16)
    router_back = jnp.dot(pick_table, w_sel.T, preferred_element_type=jnp.float32)
    sel_grad = jnp.dot(current.T, pick_table, preferred_element_type=jnp.float32)
    new_cot = (cot_wide + grad_state + router_back).astype(jnp.bfloat16)
    return new_cot, grads_up, grads_down, sel_grad


def reference(tokens, picks, halting, w_sel, w_up, w_down, cotangent):
    states = [tokens]
    kept = []
    for pass_id in range(PASSES):
        current = states[-1]
        chosen = picks[pass_id].astype(jnp.int32)
        logits = jnp.take_along_axis(jnp.dot(current, w_sel, preferred_element_type=jnp.float32), chosen, axis=1)
        gate_prob = jax.nn.sigmoid(logits)
        active = (halting > pass_id).astype(jnp.float32)
        weights_tk = active[:, None] * gate_prob
        kept.append((current, chosen, weights_tk, active, gate_prob))
        states.append(forward_pass(current, chosen, weights_tk, w_up, w_down))
    layer_out = states[-1]
    cot_now = cotangent
    d_up = jnp.zeros(w_up.shape, jnp.float32)
    d_down = jnp.zeros(w_down.shape, jnp.float32)
    d_sel = jnp.zeros(w_sel.shape, jnp.float32)
    for pass_id in reversed(range(PASSES)):
        current, chosen, weights_tk, active, gate_prob = kept[pass_id]
        cot_now, grads_up, grads_down, sel_grad = backward_pass(current, chosen, weights_tk, active, gate_prob, cot_now, w_up, w_down, w_sel)
        d_up = d_up + grads_up
        d_down = d_down + grads_down
        d_sel = d_sel + sel_grad
    return (layer_out, cot_now, d_up, d_down, d_sel)
```

```python
import jax
import jax.numpy as jnp
from jax import lax
from jax.experimental import pallas as pl
from jax.experimental.pallas import tpu as pltpu
from jax.sharding import PartitionSpec as P

BF = jnp.bfloat16
F32 = jnp.float32
GELU_C = 0.7978845608028654
GELU_A = 0.044715

TOK = 128
HALF = 256
HID = 256
NE = 8
CAP = 10
GRP = 8
GROUPS = 4
GTOK = GRP * TOK
GSLOT = GRP * CAP
ESLOT = GROUPS * GSLOT
OWN = 2 * ESLOT
EXT = 16
VMEM = pl.BlockSpec(memory_space=pltpu.VMEM)
SMEM = pl.BlockSpec(memory_space=pltpu.SMEM)


def dev(x, z, c):
    return (x * 4 + z) * 2 + c


PLACES = [(x, z, c) for x in range(4) for z in range(4) for c in range(2)]
SWAP = [(dev(x, z, c), dev(x, z, 1 - c)) for x, z, c in PLACES]


def along(axis, step):
    pairs = []
    for x, z, c in PLACES:
        if (axis + c) % 2 == 1:
            pairs.append((dev(x, z, c), dev((x + step) % 4, z, c)))
        else:
            pairs.append((dev(x, z, c), dev(x, (z + step) % 4, c)))
    return pairs


def hop(value, axis, step):
    return lax.ppermute(value, "expert", along(axis, step % 4))


def swap(value):
    return lax.ppermute(value, "expert", SWAP)


def hop_dp(value, step):
    return lax.ppermute(value, "dp", [(y, (y + step) % 4) for y in range(4)])


def call(body, outs, ins, flops=0, bytes_accessed=1 << 20, scratch=(), smem=0, limit=56):
    return pl.pallas_call(
        body,
        out_shape=outs,
        in_specs=[SMEM] * smem + [VMEM] * (len(ins) - smem),
        out_specs=jax.tree.map(lambda _: VMEM, outs),
        scratch_shapes=list(scratch),
        compiler_params=pltpu.CompilerParams(vmem_limit_bytes=limit * 1024 * 1024),
        cost_estimate=pl.CostEstimate(flops=flops, bytes_accessed=bytes_accessed, transcendentals=0),
    )(*ins)


def shape(dims, dtype):
    return jax.ShapeDtypeStruct(dims, dtype)


def mm(a, b):
    return lax.dot_general(a, b, (((1,), (0,)), ((), ())), preferred_element_type=F32)


def mm_nt(a, b):
    return lax.dot_general(a, b, (((1,), (1,)), ((), ())), preferred_element_type=F32)


def mm_tn(a, b):
    return lax.dot_general(a, b, (((0,), (0,)), ((), ())), preferred_element_type=F32)


def routing_body(eid_ref, *refs):
    own, (v_ref, vt_ref) = refs[:4], refs[4:]
    eid = eid_ref[:, :]
    marks = []
    for g in range(GROUPS):
        for j in range(GRP):
            named = own[g][GTOK + 16 * j : GTOK + 16 * j + 16, :].astype(F32)
            mark = jnp.zeros((NE, 256), F32)
            for k in range(16):
                mark = jnp.where(named[k : k + 1, :] == eid, 1.0, mark)
            marks.append(mark)
    before = lax.broadcasted_iota(jnp.int32, (TOK, TOK), 0) < lax.broadcasted_iota(jnp.int32, (TOK, TOK), 1)
    before = jnp.where(before, 1.0, 0.0).astype(BF)
    for p in range(2):
        stacked = jnp.concatenate([m[:, p * TOK : (p + 1) * TOK] for m in marks], axis=0)
        rank = mm(stacked.astype(BF), before)
        for g in range(GROUPS):
            rows = []
            for j in range(GRP):
                at = (g * GRP + j) * NE
                rows.append(jnp.where(stacked[at : at + NE] > 0, rank[at : at + NE] + float(CAP * j), -1.0))
            v = jnp.concatenate(rows, axis=1)
            v_ref[p, g] = v
            padded = jnp.concatenate([v, jnp.zeros((TOK - NE, GTOK), F32)], axis=0)
            vt_ref[p, g] = padded.T.astype(BF)


def gather_rows(v_ref, own, oth, x_ref):
    slot = lax.broadcasted_iota(jnp.int32, (GSLOT, GTOK), 0).astype(F32)
    for g in range(GROUPS):
        v = v_ref[g]
        pick = jnp.concatenate([jnp.where(slot == v[e : e + 1, :], 1.0, 0.0).astype(BF) for e in range(NE)], axis=0)
        near = own[g][0:GTOK, :]
        far = jnp.concatenate(
            [
                oth[d1][(g * 2 + 1 - dc) * TOK : (g * 2 + 2 - dc) * TOK, :]
                for d1 in range(4)
                for dc in range(2)
            ],
            axis=0,
        )
        for h, source in enumerate((near, far)):
            rows = mm(pick, source).astype(BF)
            for e in range(NE):
                x_ref[e, g * GSLOT : (g + 1) * GSLOT, h * HALF : (h + 1) * HALF] = rows[e * GSLOT : (e + 1) * GSLOT]


def halves(sc_ref):
    core = sc_ref[1]
    return (
        pl.ds(pl.multiple_of(core * HALF, HALF), HALF),
        pl.ds(pl.multiple_of((1 - core) * HALF, HALF), HALF),
    )


def expert_at(sc_ref, e):
    return lax.rem(2 * sc_ref[0] + e, NE)


def up_body(sc_ref, v_ref, w_up_ref, sel_ref, *refs):
    own, oth, x_ref, parts = refs[0:4], refs[4:8], refs[8], refs[9:13]
    gather_rows(v_ref, own, oth, x_ref)
    first, second = halves(sc_ref)
    sel = sel_ref[:, :]
    lane_pad = jnp.zeros((1, 192), F32)
    for dy in range(4):
        heads, tails = [], []
        for i in range(2):
            e = 2 * dy + i
            at = expert_at(sc_ref, e)
            rows = x_ref[e]
            total = mm(rows[:, :HALF], w_up_ref[at, first, :]) + mm(rows[:, HALF:], w_up_ref[at, second, :])
            parts[dy][i * ESLOT : (i + 1) * ESLOT, :] = total.astype(BF)
            logit = mm_nt(sel, rows)[e : e + 1, :]
            heads.append(logit[:, :256])
            tails.append(jnp.concatenate([logit[:, 256:], lane_pad], axis=1))
        logits = jnp.concatenate(heads + tails, axis=0)
        high = logits.astype(BF).astype(F32)
        low = logits - high
        parts[dy][OWN:, :] = jnp.concatenate([high, low, jnp.zeros((8, 256), F32)], axis=0).astype(BF)


def down_grad_body(sc_ref, v_ref, w_down_ref, *refs):
    own, oth, x_ref, parts = refs[0:4], refs[4:8], refs[8], refs[9:13]
    gather_rows(v_ref, own, oth, x_ref)
    first, second = halves(sc_ref)
    for e in range(NE):
        at = expert_at(sc_ref, e)
        rows = x_ref[e]
        total = mm_nt(rows[:, :HALF], w_down_ref[at, :, first]) + mm_nt(rows[:, HALF:], w_down_ref[at, :, second])
        parts[e // 2][(e % 2) * ESLOT : (e % 2 + 1) * ESLOT, :] = total.astype(BF)


def as_columns(rows):
    turned = jnp.concatenate([rows, jnp.zeros((TOK - rows.shape[0], 256), F32)], axis=0).T
    return jnp.concatenate([turned[:, 0:1], turned[:64, 2:3], turned[:, 1:2], turned[:64, 3:4]], axis=0)


def as_rows(column):
    wide = jnp.broadcast_to(column, (OWN, TOK))
    lane = lax.broadcasted_iota(jnp.int32, (256, TOK), 1)
    pad = jnp.zeros((192, TOK), F32)
    pieces = (
        wide[0:256],
        wide[ESLOT : ESLOT + 256],
        jnp.concatenate([wide[256:ESLOT], pad], axis=0),
        jnp.concatenate([wide[ESLOT + 256 :], pad], axis=0),
    )
    mixed = jnp.zeros((256, TOK), F32)
    for i, piece in enumerate(pieces):
        mixed = jnp.where(lane == i, piece, mixed)
    return mixed.T[:EXT]


def settle_body(p0, p1, p2, p3, hid_ref, pre_ref, gate_ref):
    def total(lo, hi):
        return sum(p[lo:hi, :].astype(F32) for p in (p0, p1, p2, p3))

    extra = total(OWN, OWN + EXT)
    gate = jax.nn.sigmoid(as_columns(extra[0:4] + extra[4:8]))
    pre = total(0, OWN)
    pre_ref[:, :] = pre
    gate_ref[:, :] = jnp.broadcast_to(gate, (OWN, TOK))
    inner = GELU_C * (pre + GELU_A * pre * pre * pre)
    hid_ref[:, :] = (gate * (0.5 * pre * (1.0 + jnp.tanh(inner)))).astype(BF)


def settle_grad_body(p0, p1, p2, p3, pre_ref, gate_ref, grad_ref):
    total = sum(p[:, :].astype(F32) for p in (p0, p1, p2, p3))
    pre = pre_ref[:, :]
    gate = gate_ref[:, 0:1]
    tangent = jnp.tanh(GELU_C * (pre + GELU_A * pre * pre * pre))
    hidden = (0.5 * pre * (1.0 + tangent)).astype(BF).astype(F32)
    slope = 0.5 * (1.0 + tangent) + 0.5 * pre * (1.0 - tangent * tangent) * GELU_C * (1.0 + 3.0 * GELU_A * pre * pre)
    score = jnp.sum(hidden * total, axis=1, keepdims=True)
    grad_ref[0:OWN, :] = (gate * total * slope).astype(BF)
    grad_ref[OWN:, :] = as_rows(score * gate * (1.0 - gate)).astype(BF)


def scatter_rows(vt_ref, out_ref, own_ref, oth_ref):
    at_lane = lax.broadcasted_iota(jnp.int32, (TOK, NE * GSLOT), 1)
    at_row = lax.broadcasted_iota(jnp.int32, (TOK, NE * GSLOT), 0)
    spread = jnp.where((at_lane >= at_row * GSLOT) & (at_lane < (at_row + 1) * GSLOT), 1.0, 0.0).astype(BF)
    lane = lax.broadcasted_iota(jnp.int32, (1, NE * GSLOT), 1)
    slot = lax.rem(lane, GSLOT).astype(F32)
    for g in range(GROUPS):
        put = jnp.where(mm(vt_ref[g], spread) == slot, 1.0, 0.0).astype(BF)
        far = mm(put, out_ref[g, :, HALF:]).astype(BF)
        for d1 in range(4):
            for dc in range(2):
                j = d1 * 2 + dc
                to = (d1 * 8 + g * 2 + 1 - dc) * TOK
                oth_ref[to : to + TOK, :] = far[j * TOK : (j + 1) * TOK]
        own_ref[g * GTOK : (g + 1) * GTOK, :] = mm(put, out_ref[g, :, :HALF]).astype(BF)


def down_body(sc_ref, vt_ref, w_down_ref, h0, h1, h2, h3, own_ref, oth_ref, out_ref):
    hid = (h0, h1, h2, h3)
    first, second = halves(sc_ref)
    for e in range(NE):
        at = expert_at(sc_ref, e)
        rows = hid[e // 2][(e % 2) * ESLOT : (e % 2 + 1) * ESLOT, :]
        for h, cols in enumerate((first, second)):
            out = mm(rows, w_down_ref[at, :, cols]).astype(BF)
            for g in range(GROUPS):
                out_ref[g, e * GSLOT : (e + 1) * GSLOT, h * HALF : (h + 1) * HALF] = out[g * GSLOT : (g + 1) * GSLOT]
    scatter_rows(vt_ref, out_ref, own_ref, oth_ref)


def logit_rows(grads):
    rows = []
    for piece in grads:
        extra = piece[OWN:, :].astype(F32)
        for i in range(2):
            rows.append(jnp.concatenate([extra[i : i + 1, :], extra[2 + i : 3 + i, :64]], axis=1))
    return jnp.concatenate(rows, axis=0)


def up_grad_body(sc_ref, vt_ref, w_up_ref, sel_ref, h0, h1, h2, h3, own_ref, oth_ref, out_ref):
    grads = (h0, h1, h2, h3)
    first, second = halves(sc_ref)
    sel = sel_ref[:, :].astype(F32)
    rows = logit_rows(grads)
    rows = jnp.concatenate([rows, jnp.zeros((NE, 64), F32)], axis=1)
    columns = jnp.concatenate([rows, jnp.zeros((TOK - NE, 384), F32)], axis=0).T
    for e in range(NE):
        at = expert_at(sc_ref, e)
        grad = grads[e // 2][(e % 2) * ESLOT : (e % 2 + 1) * ESLOT, :]
        logit_grad = columns[:ESLOT, e : e + 1]
        for h, cols in enumerate((first, second)):
            out = mm_nt(grad, w_up_ref[at, cols, :])
            out = (out + logit_grad * sel[e : e + 1, h * HALF : (h + 1) * HALF]).astype(BF)
            for g in range(GROUPS):
                out_ref[g, e * GSLOT : (e + 1) * GSLOT, h * HALF : (h + 1) * HALF] = out[g * GSLOT : (g + 1) * GSLOT]
    scatter_rows(vt_ref, out_ref, own_ref, oth_ref)


def d_down_body(sc_ref, c0_ref, c1_ref, *refs):
    hid, d_ref = (refs[0:4], refs[4:8]), refs[8]
    first, second = halves(sc_ref)
    for e in range(NE):
        at = expert_at(sc_ref, e)
        span = slice((e % 2) * ESLOT, (e % 2 + 1) * ESLOT)
        for h, cols in enumerate((first, second)):
            part = slice(h * HALF, (h + 1) * HALF)
            d_ref[at, :, cols] = mm_tn(hid[0][e // 2][span, :], c0_ref[e, :, part]) + mm_tn(
                hid[1][e // 2][span, :], c1_ref[e, :, part]
            )


def d_up_body(sc_ref, x0_ref, x1_ref, *refs):
    grads, d_ref, sel_ref = (refs[0:4], refs[4:8]), refs[8], refs[9]
    first, second = halves(sc_ref)
    rows = [logit_rows(grads[p]).astype(BF) for p in range(2)]
    for e in range(NE):
        at = expert_at(sc_ref, e)
        span = slice((e % 2) * ESLOT, (e % 2 + 1) * ESLOT)
        for h, cols in enumerate((first, second)):
            part = slice(h * HALF, (h + 1) * HALF)
            d_ref[at, cols, :] = mm_tn(x0_ref[e, :, part], grads[0][e // 2][span, :]) + mm_tn(
                x1_ref[e, :, part], grads[1][e // 2][span, :]
            )
            d_sel = mm(rows[0], x0_ref[e, :, part]) + mm(rows[1], x1_ref[e, :, part])
            sel_ref[pl.ds(at, 1), cols] = d_sel[e : e + 1, :]


def add_swapped_body(own_ref, got_ref, *outs):
    for g in range(GROUPS):
        span = slice(g * GTOK, (g + 1) * GTOK)
        outs[g][:, :] = (own_ref[span, :].astype(F32) + got_ref[span, :].astype(F32)).astype(BF)


def add_second_body(a, b, c, d, *outs):
    for i in range(4):
        span = slice(i * 256, (i + 1) * 256)
        outs[i][:, :] = sum(r[span, :].astype(F32) for r in (a, b, c, d)).astype(BF)


def gather_chip(mine, extra=None):
    pieces = [mine] + [hop(mine, 1, -d) for d in (1, 2, 3)]
    rows = 2 * TOK
    stacked = jnp.concatenate([q[:rows] for q in pieces] + [q[rows:] for q in pieces if q.shape[0] > rows], axis=0)
    own = [stacked] + [hop(stacked, 2, -d) for d in (1, 2, 3)]
    oth = [swap(q[:GTOK]) for q in own]
    return own, oth


def scatter_chip(own, oth):
    outs = [shape((GTOK, HALF), BF)] * 4
    second = call(add_swapped_body, outs, (own, swap(oth)), bytes_accessed=6 << 20)
    got = [second[0]] + [hop(second[d], 2, d) for d in (1, 2, 3)]
    first = call(add_second_body, [shape((2 * TOK, HALF), BF)] * 4, got, bytes_accessed=3 << 20)
    return [first[0]] + [hop(first[d], 1, d) for d in (1, 2, 3)]


def all_dp(block):
    return [block] + [hop_dp(block, -d) for d in (1, 2, 3)]


def to_dp(parts):
    return [parts[0]] + [hop_dp(parts[d], d) for d in (1, 2, 3)]


def per_device(tokens, picks, halting, w_sel, w_up, w_down, cotangent):
    dp = lax.axis_index("dp")
    place = lax.axis_index("expert")
    core = lax.rem(place, 2)
    sc = jnp.stack([dp, core]).astype(jnp.int32)
    rel = lax.rem(2 * dp + jnp.arange(NE, dtype=jnp.int32), NE) + NE * place
    eid = jnp.broadcast_to(rel.astype(F32)[:, None], (NE, 256))
    sel = w_sel.T[rel]
    sel = jnp.where(core == 0, sel, jnp.concatenate([sel[:, HALF:], sel[:, :HALF]], axis=1))

    def mine_of(array):
        return jnp.where(core == 0, array[:, :HALF], array[:, HALF:])

    def rest_of(array):
        return jnp.where(core == 0, array[:, HALF:], array[:, :HALF])

    live = halting[None, :, None] > jnp.arange(2, dtype=jnp.int32)[:, None, None]
    named = jnp.where(live, picks, 256).transpose(2, 0, 1).reshape(16, 256).astype(BF)
    rest = swap(jnp.concatenate([rest_of(tokens), named], axis=0))
    state = jnp.concatenate([mine_of(tokens), rest[:TOK]], axis=0)
    cot = jnp.concatenate([mine_of(cotangent), swap(rest_of(cotangent))], axis=0)

    own, oth = gather_chip(jnp.concatenate([state, named, rest[TOK:]], axis=0))
    v, vt = call(
        routing_body,
        [shape((2, GROUPS, NE, GTOK), F32), shape((2, GROUPS, GTOK, TOK), BF)],
        (eid, *own),
        bytes_accessed=6 << 20,
    )

    rows_type = shape((NE, ESLOT, 2 * HALF), BF)
    gather_flops = 2 * 640 * 1024 * 512 * 4 + 2 * 2560 * 512 * 256

    def project_up(p, own, oth):
        outs = [rows_type] + [shape((OWN + EXT, HID), BF)] * 4
        return call(
            up_body, outs, (sc, v[p], w_up, sel, *own, *oth), flops=gather_flops, bytes_accessed=12 << 20, smem=1
        )

    def project_cot(p, own, oth):
        outs = [rows_type] + [shape((OWN, HID), BF)] * 4
        return call(
            down_grad_body, outs, (sc, v[p], w_down, *own, *oth), flops=gather_flops, bytes_accessed=12 << 20, smem=1
        )

    def settle(parts):
        outs = [shape((OWN, HID), BF), shape((OWN, HID), F32), shape((OWN, TOK), F32)]
        return call(settle_body, outs, to_dp(parts), bytes_accessed=3 << 20)

    def settle_grad(parts, pre, gate):
        return call(settle_grad_body, shape((OWN + EXT, HID), BF), (*parts, pre, gate), bytes_accessed=3 << 20)

    spread = [shape((GROUPS * GTOK, HALF), BF)] * 2
    out_scratch = [pltpu.VMEM((GROUPS, NE * GSLOT, 2 * HALF), BF)]

    def outputs(p, hid):
        return call(
            down_body,
            spread,
            (sc, vt[p], w_down, *hid),
            flops=gather_flops,
            bytes_accessed=10 << 20,
            scratch=out_scratch,
            smem=1,
        )

    def grads_in(p, grads):
        return call(
            up_grad_body,
            spread,
            (sc, vt[p], w_up, sel, *grads),
            flops=gather_flops,
            bytes_accessed=10 << 20,
            scratch=out_scratch,
            smem=1,
        )

    def advance(base, terms):
        return (base.astype(F32) + sum(t.astype(F32) for t in terms)).astype(BF)

    x0, *parts = project_up(0, own, oth)
    hid0, pre0, gate0 = settle(parts)
    c1, *cot_parts = project_cot(1, *gather_chip(cot))
    cot_parts = to_dp(cot_parts)
    hid0 = all_dp(hid0)
    state1 = advance(state, scatter_chip(*outputs(0, hid0)))

    own, oth = gather_chip(state1)
    x1, *parts = project_up(1, own, oth)
    hid1, pre1, gate1 = settle(parts)
    grad1 = all_dp(settle_grad(cot_parts, pre1, gate1))
    hid1 = all_dp(hid1)

    cot1 = advance(cot, scatter_chip(*grads_in(1, grad1)))
    state2 = advance(state1, scatter_chip(*outputs(1, hid1)))

    c0, *cot_parts = project_cot(0, *gather_chip(cot1))
    grad0 = all_dp(settle_grad(to_dp(cot_parts), pre0, gate0))
    d_down = call(
        d_down_body,
        shape(w_down.shape, F32),
        (sc, c0, c1, *hid0, *hid1),
        flops=4 * 2560 * 512 * 256,
        bytes_accessed=16 << 20,
        smem=1,
    )
    cot0 = advance(cot1, scatter_chip(*grads_in(0, grad0)))
    d_up, d_sel = call(
        d_up_body,
        [shape(w_up.shape, F32), shape((NE, 2 * HALF), F32)],
        (sc, x0, x1, *grad0, *grad1),
        flops=4 * 2560 * 512 * 256,
        bytes_accessed=16 << 20,
        smem=1,
    )
    d_sel = lax.all_gather(d_sel, "expert", axis=0, tiled=True).T

    def whole(array):
        mine, rest = array[:TOK], swap(array[TOK:])
        return jnp.where(
            core == 0, jnp.concatenate([mine, rest], axis=1), jnp.concatenate([rest, mine], axis=1)
        )

    return (whole(state2), whole(cot0), d_up, d_down, d_sel)


def solution(mesh):
    in_specs = (
        P("expert", "dp"),
        P(None, "expert", None),
        P("expert"),
        P("dp", None),
        P("expert", "dp", None),
        P("expert", None, "dp"),
        P("expert", "dp"),
    )
    out_specs = (
        P("expert", "dp"),
        P("expert", "dp"),
        P("expert", "dp", None),
        P("expert", None, "dp"),
        P("dp", None),
    )
    return jax.shard_map(
        per_device, mesh=mesh, in_specs=in_specs, out_specs=out_specs, check_vma=False
    )
```

```python
import functools

import jax
import jax.numpy as jnp
from jax import lax
from jax.experimental import pallas as pl
from jax.experimental.pallas import tpu as pltpu
from jax.sharding import PartitionSpec as P

BF = jnp.bfloat16
F32 = jnp.float32
GELU_C = 0.7978845608028654
GELU_A = 0.044715

TOK = 128
HALF = 256
HID = 256
NE = 8
CAP = 10
GRP = 8
GROUPS = 4
GTOK = GRP * TOK
GSLOT = GRP * CAP
ESLOT = GROUPS * GSLOT
OWN = 2 * ESLOT
EXT = 16
QUADS = 8
QTOK = 4 * TOK
QCAP = 4 * CAP
QSLOT = NE * QCAP
EXPERTS = 256
VMEM = pl.BlockSpec(memory_space=pltpu.VMEM)
HBM = pl.BlockSpec(memory_space=pl.ANY)
SMEM = pl.BlockSpec(memory_space=pltpu.SMEM)


def dev(x, z, c):
    return (x * 4 + z) * 2 + c


PLACES = [(x, z, c) for x in range(4) for z in range(4) for c in range(2)]
SWAP = [(dev(x, z, c), dev(x, z, 1 - c)) for x, z, c in PLACES]


def along(axis, step):
    pairs = []
    for x, z, c in PLACES:
        if (axis + c) % 2 == 1:
            pairs.append((dev(x, z, c), dev((x + step) % 4, z, c)))
        else:
            pairs.append((dev(x, z, c), dev(x, (z + step) % 4, c)))
    return pairs


def hop(value, axis, step):
    return lax.ppermute(value, "expert", along(axis, step % 4))


def swap(value):
    return lax.ppermute(value, "expert", SWAP)


def hop_dp(value, step):
    return lax.ppermute(value, "dp", [(y, (y + step) % 4) for y in range(4)])


def call(body, outs, ins, flops=0, moved=1 << 20, scratch=(), smem=0, anywhere=0, outs_anywhere=(), limit=48):
    flat = [outs] if not isinstance(outs, list) else outs
    specs = [HBM if i in outs_anywhere else VMEM for i in range(len(flat))]
    return pl.pallas_call(
        body,
        out_shape=outs,
        in_specs=[SMEM] * smem + [VMEM] * (len(ins) - smem - anywhere) + [HBM] * anywhere,
        out_specs=specs if isinstance(outs, list) else specs[0],
        scratch_shapes=list(scratch),
        compiler_params=pltpu.CompilerParams(vmem_limit_bytes=limit * 1024 * 1024),
        cost_estimate=pl.CostEstimate(flops=flops, bytes_accessed=moved, transcendentals=0),
    )(*ins)


def shape(dims, dtype):
    return jax.ShapeDtypeStruct(dims, dtype)


def tie(*values):
    return lax.optimization_barrier(values)


def mm(a, b):
    return lax.dot_general(a, b, (((1,), (0,)), ((), ())), preferred_element_type=F32)


def mm_nt(a, b):
    return lax.dot_general(a, b, (((1,), (1,)), ((), ())), preferred_element_type=F32)


def mm_tn(a, b):
    return lax.dot_general(a, b, (((0,), (0,)), ((), ())), preferred_element_type=F32)


def started(copies):
    for copy in copies:
        copy.start()
    return copies


def routing_body(eid_ref, own0, own1, own2, own3, v_ref, named_ref, sems):
    loads = started(
        [
            pltpu.make_async_copy(own.at[GTOK : GTOK + 16 * GRP], named_ref.at[g], sems.at[g])
            for g, own in enumerate((own0, own1, own2, own3))
        ]
    )
    eid = eid_ref[:, :]
    marks = []
    for g in range(GROUPS):
        loads[g].wait()
        for j in range(GRP):
            named = named_ref[g, 16 * j : 16 * j + 16, :].astype(F32)
            mark = jnp.zeros((NE, 256), F32)
            for k in range(16):
                mark = jnp.where(named[k : k + 1, :] == eid, 1.0, mark)
            marks.append(mark)
    before = lax.broadcasted_iota(jnp.int32, (TOK, TOK), 0) < lax.broadcasted_iota(jnp.int32, (TOK, TOK), 1)
    before = jnp.where(before, 1.0, 0.0).astype(BF)
    for p in range(2):
        stacked = jnp.concatenate([m[:, p * TOK : (p + 1) * TOK] for m in marks], axis=0)
        rank = mm(stacked.astype(BF), before)
        for g in range(GROUPS):
            for j in range(GRP):
                at = (g * GRP + j) * NE
                v_ref[p, g, :, j * TOK : (j + 1) * TOK] = jnp.where(
                    stacked[at : at + NE] > 0, rank[at : at + NE] + float(CAP * (j % 4)), -1.0
                )


def put_body(v_ref, put_ref):
    at_lane = lax.broadcasted_iota(jnp.int32, (TOK, QSLOT), 1)
    at_row = lax.broadcasted_iota(jnp.int32, (TOK, QSLOT), 0)
    spread = jnp.where((at_lane >= at_row * QCAP) & (at_lane < (at_row + 1) * QCAP), 1.0, 0.0).astype(BF)
    slot = lax.rem(lax.broadcasted_iota(jnp.int32, (1, QSLOT), 1), QCAP).astype(F32)
    for q in range(QUADS):
        v = v_ref[q // 2, :, (q % 2) * QTOK : (q % 2 + 1) * QTOK]
        turned = jnp.concatenate([v, jnp.zeros((TOK - NE, QTOK), F32)], axis=0).T.astype(BF)
        put_ref[q] = jnp.where(mm(turned, spread) == slot, 1.0, 0.0).astype(BF)


def gather_rows(v_ref, own, oth, near_ref, far_ref, x_ref, sems):
    near = [pltpu.make_async_copy(own[g].at[0:GTOK], near_ref.at[g], sems.at[g]) for g in range(GROUPS)]
    far = [
        [
            pltpu.make_async_copy(
                oth[d].at[g * 256 : (g + 1) * 256], far_ref.at[g, d * 256 : (d + 1) * 256], sems.at[4 + 4 * g + d]
            )
            for d in range(4)
        ]
        for g in range(GROUPS)
    ]
    for g in range(GROUPS):
        near[g].start()
        started(far[g])
    slot = lax.broadcasted_iota(jnp.int32, (QCAP, QTOK), 0).astype(F32)
    for g in range(GROUPS):
        near[g].wait()
        for copy in far[g]:
            copy.wait()
        rows = []
        for i in range(2):
            span = slice(i * QTOK, (i + 1) * QTOK)
            v = v_ref[g, :, span]
            pick = jnp.concatenate([jnp.where(slot == v[e : e + 1, :], 1.0, 0.0) for e in range(NE)], axis=0).astype(BF)
            rows.append((mm(pick, near_ref[g, span, :]), mm(pick, far_ref[g, span, :])))
        for e in range(NE):
            at = slice(e * QCAP, (e + 1) * QCAP)
            for h in range(2):
                x_ref[e, g * GSLOT : (g + 1) * GSLOT, h * HALF : (h + 1) * HALF] = jnp.concatenate(
                    [rows[0][h][at], rows[1][h][at]], axis=0
                ).astype(BF)


def halves(sc_ref):
    core = sc_ref[1]
    return (
        pl.ds(pl.multiple_of(core * HALF, HALF), HALF),
        pl.ds(pl.multiple_of((1 - core) * HALF, HALF), HALF),
    )


def expert_at(sc_ref, e):
    return lax.rem(2 * sc_ref[0] + e, NE)


def up_body(sc_ref, v_ref, sel_ref, w_hbm, *refs):
    own, oth, x_hbm, parts = refs[0:4], refs[4:8], refs[8], refs[9:13]
    near_ref, far_ref, x_ref, w_up_ref, sems, w_sem, x_sem = refs[13:]
    load = pltpu.make_async_copy(w_hbm, w_up_ref, w_sem)
    load.start()
    gather_rows(v_ref, own, oth, near_ref, far_ref, x_ref, sems)
    store = pltpu.make_async_copy(x_ref, x_hbm, x_sem)
    store.start()
    load.wait()
    first, second = halves(sc_ref)
    sel = sel_ref[:, :]
    lane_pad = jnp.zeros((1, 192), F32)
    for dy in range(4):
        heads, tails = [], []
        for i in range(2):
            e = 2 * dy + i
            at = expert_at(sc_ref, e)
            rows = x_ref[e]
            total = mm(rows[:, :HALF], w_up_ref[at, first, :]) + mm(rows[:, HALF:], w_up_ref[at, second, :])
            parts[dy][i * ESLOT : (i + 1) * ESLOT, :] = total.astype(BF)
            logit = mm_nt(sel, rows)[e : e + 1, :]
            heads.append(logit[:, :256])
            tails.append(jnp.concatenate([logit[:, 256:], lane_pad], axis=1))
        logits = jnp.concatenate(heads + tails, axis=0)
        high = logits.astype(BF).astype(F32)
        low = logits - high
        parts[dy][OWN:, :] = jnp.concatenate([high, low, jnp.zeros((8, 256), F32)], axis=0).astype(BF)
    store.wait()


def down_grad_body(sc_ref, v_ref, w_hbm, *refs):
    own, oth, x_hbm, parts = refs[0:4], refs[4:8], refs[8], refs[9:13]
    near_ref, far_ref, x_ref, w_down_ref, sems, w_sem, x_sem = refs[13:]
    load = pltpu.make_async_copy(w_hbm, w_down_ref, w_sem)
    load.start()
    gather_rows(v_ref, own, oth, near_ref, far_ref, x_ref, sems)
    store = pltpu.make_async_copy(x_ref, x_hbm, x_sem)
    store.start()
    load.wait()
    first, second = halves(sc_ref)
    for e in range(NE):
        at = expert_at(sc_ref, e)
        rows = x_ref[e]
        total = mm_nt(rows[:, :HALF], w_down_ref[at, :, first]) + mm_nt(rows[:, HALF:], w_down_ref[at, :, second])
        parts[e // 2][(e % 2) * ESLOT : (e % 2 + 1) * ESLOT, :] = total.astype(BF)
    store.wait()


def as_columns(rows):
    turned = jnp.concatenate([rows, jnp.zeros((TOK - rows.shape[0], 256), F32)], axis=0).T
    return jnp.concatenate([turned[:, 0:1], turned[:64, 2:3], turned[:, 1:2], turned[:64, 3:4]], axis=0)


def as_rows(column):
    wide = jnp.broadcast_to(column, (OWN, TOK))
    lane = lax.broadcasted_iota(jnp.int32, (256, TOK), 1)
    pad = jnp.zeros((192, TOK), F32)
    pieces = (
        wide[0:256],
        wide[ESLOT : ESLOT + 256],
        jnp.concatenate([wide[256:ESLOT], pad], axis=0),
        jnp.concatenate([wide[ESLOT + 256 :], pad], axis=0),
    )
    mixed = jnp.zeros((256, TOK), F32)
    for i, piece in enumerate(pieces):
        mixed = jnp.where(lane == i, piece, mixed)
    return mixed.T[:EXT]


def settle_body(p0, p1, p2, p3, hid_ref, pre_ref, gate_ref):
    def total(lo, hi):
        return sum(p[lo:hi, :].astype(F32) for p in (p0, p1, p2, p3))

    extra = total(OWN, OWN + EXT)
    gate = jax.nn.sigmoid(as_columns(extra[0:4] + extra[4:8]))
    pre = total(0, OWN)
    pre_ref[:, :] = pre
    gate_ref[:, :] = jnp.broadcast_to(gate, (OWN, TOK))
    inner = GELU_C * (pre + GELU_A * pre * pre * pre)
    hid_ref[:, :] = (gate * (0.5 * pre * (1.0 + jnp.tanh(inner)))).astype(BF)


def settle_grad_body(p0, p1, p2, p3, pre_ref, gate_ref, grad_ref):
    total = sum(p[:, :].astype(F32) for p in (p0, p1, p2, p3))
    pre = pre_ref[:, :]
    gate = gate_ref[:, 0:1]
    tangent = jnp.tanh(GELU_C * (pre + GELU_A * pre * pre * pre))
    hidden = (0.5 * pre * (1.0 + tangent)).astype(BF).astype(F32)
    slope = 0.5 * (1.0 + tangent) + 0.5 * pre * (1.0 - tangent * tangent) * GELU_C * (1.0 + 3.0 * GELU_A * pre * pre)
    score = jnp.sum(hidden * total, axis=1, keepdims=True)
    grad_ref[0:OWN, :] = (gate * total * slope).astype(BF)
    grad_ref[OWN:, :] = as_rows(score * gate * (1.0 - gate)).astype(BF)


def place_rows(out_ref, e, pair):
    for q in range(QUADS):
        span = slice(q * QCAP, (q + 1) * QCAP)
        out_ref[q, e * QCAP : (e + 2) * QCAP, :] = jnp.concatenate([pair[0][span], pair[1][span]], axis=0).astype(BF)


def scatter_rows(put_hbm, put_ref, loads, out_ref, y_hbm, y_ref, y_sems, far):
    stores = []
    for q in range(QUADS):
        loads[q].wait()
        rows = mm(put_ref[q], out_ref[q]).astype(BF)
        g, i = q // 2, q % 2
        for k in range(2):
            d = 2 * i + k
            at = ((d * 4 + g) if far else (g * 4 + d)) * 256
            y_ref[at : at + 256, :] = rows[k * 256 : (k + 1) * 256]
            stores.append(pltpu.make_async_copy(y_ref.at[at : at + 256], y_hbm.at[at : at + 256], y_sems.at[2 * q + k]))
            stores[-1].start()
    for copy in stores:
        copy.wait()


def load_all(sc_ref, w_view, w_ref, w_sem, hid_hbm, hid_ref, hid_sems, put_hbm, put_ref, put_sems):
    w_load = pltpu.make_async_copy(w_view, w_ref, w_sem)
    hid_loads = [pltpu.make_async_copy(hid_hbm[d], hid_ref.at[d], hid_sems.at[d]) for d in range(4)]
    put_loads = [pltpu.make_async_copy(put_hbm.at[q], put_ref.at[q], put_sems.at[q]) for q in range(QUADS)]
    hid_loads[0].start()
    w_load.start()
    started(hid_loads[1:])
    started(put_loads)
    w_load.wait()
    return hid_loads, put_loads


def down_body(far, sc_ref, put_hbm, w_hbm, h0, h1, h2, h3, y_hbm, y_ref, out_ref, w_ref, hid_ref, put_ref, w_sem, hid_sems, put_sems, y_sems):
    cols = halves(sc_ref)[1 if far else 0]
    hid_loads, put_loads = load_all(
        sc_ref, w_hbm.at[:, :, cols], w_ref, w_sem, (h0, h1, h2, h3), hid_ref, hid_sems, put_hbm, put_ref, put_sems
    )
    for d in range(4):
        hid_loads[d].wait()
        pair = [
            mm(hid_ref[d, i * ESLOT : (i + 1) * ESLOT, :], w_ref[expert_at(sc_ref, 2 * d + i)]) for i in range(2)
        ]
        place_rows(out_ref, 2 * d, pair)
    scatter_rows(put_hbm, put_ref, put_loads, out_ref, y_hbm, y_ref, y_sems, far)


def logit_rows(extras):
    rows = []
    for extra in extras:
        extra = extra.astype(F32)
        for i in range(2):
            rows.append(jnp.concatenate([extra[i : i + 1, :], extra[2 + i : 3 + i, :64]], axis=1))
    return jnp.concatenate(rows, axis=0)


def up_grad_body(far, sc_ref, sel_ref, put_hbm, w_hbm, h0, h1, h2, h3, y_hbm, y_ref, out_ref, w_ref, hid_ref, put_ref, w_sem, hid_sems, put_sems, y_sems):
    part = slice(HALF, 2 * HALF) if far else slice(0, HALF)
    rows = halves(sc_ref)[1 if far else 0]
    hid_loads, put_loads = load_all(
        sc_ref, w_hbm.at[:, rows, :], w_ref, w_sem, (h0, h1, h2, h3), hid_ref, hid_sems, put_hbm, put_ref, put_sems
    )
    sel = sel_ref[:, part].astype(F32)
    for copy in hid_loads:
        copy.wait()
    rows = logit_rows([hid_ref[d, OWN:, :] for d in range(4)])
    rows = jnp.concatenate([rows, jnp.zeros((NE, 64), F32)], axis=1)
    columns = jnp.concatenate([rows, jnp.zeros((TOK - NE, 384), F32)], axis=0).T
    for d in range(4):
        pair = []
        for i in range(2):
            e = 2 * d + i
            out = mm_nt(hid_ref[d, i * ESLOT : (i + 1) * ESLOT, :], w_ref[expert_at(sc_ref, e)])
            pair.append(out + columns[:ESLOT, e : e + 1] * sel[e : e + 1, :])
        place_rows(out_ref, 2 * d, pair)
    scatter_rows(put_hbm, put_ref, put_loads, out_ref, y_hbm, y_ref, y_sems, far)


def d_down_body(sc_ref, c0_ref, c1_ref, *refs):
    hid, d_ref = (refs[0:4], refs[4:8]), refs[8]
    first, second = halves(sc_ref)
    for e in range(NE):
        at = expert_at(sc_ref, e)
        span = slice((e % 2) * ESLOT, (e % 2 + 1) * ESLOT)
        for h, cols in enumerate((first, second)):
            part = slice(h * HALF, (h + 1) * HALF)
            d_ref[at, :, cols] = mm_tn(hid[0][e // 2][span, :], c0_ref[e, :, part]) + mm_tn(
                hid[1][e // 2][span, :], c1_ref[e, :, part]
            )


def d_up_body(sc_ref, x0_ref, x1_ref, *refs):
    grads, d_ref = (refs[0:4], refs[4:8]), refs[8]
    first, second = halves(sc_ref)
    for e in range(NE):
        at = expert_at(sc_ref, e)
        span = slice((e % 2) * ESLOT, (e % 2 + 1) * ESLOT)
        for h, cols in enumerate((first, second)):
            part = slice(h * HALF, (h + 1) * HALF)
            d_ref[at, cols, :] = mm_tn(x0_ref[e, :, part], grads[0][e // 2][span, :]) + mm_tn(
                x1_ref[e, :, part], grads[1][e // 2][span, :]
            )


def d_sel_body(sc_ref, x0_ref, x1_ref, *refs):
    grads, sel_ref = (refs[0:4], refs[4:8]), refs[8]
    first, second = halves(sc_ref)
    rows = [logit_rows([g[OWN:, :] for g in grads[p]]).astype(BF) for p in range(2)]
    for e in range(NE):
        at = expert_at(sc_ref, e)
        d_sel = (mm(rows[0], x0_ref[e]) + mm(rows[1], x1_ref[e]))[e : e + 1, :]
        sel_ref[pl.ds(at, 1), first] = d_sel[:, :HALF]
        sel_ref[pl.ds(at, 1), second] = d_sel[:, HALF:]


def d_sel_order_body(place_ref, own_ref, oth_ref, out_ref, all_ref):
    place = place_ref[0]
    x, z, core = place // 8, lax.rem(place // 2, 4), lax.rem(place, 2)
    for source, side in ((own_ref, core), (oth_ref, 1 - core)):
        for second in range(4):
            for first in range(4):
                dx = jnp.where(side == 0, first, second)
                dz = jnp.where(side == 0, second, first)
                to = ((lax.rem(x + dx, 4) * 4 + lax.rem(z + dz, 4)) * 2 + side) * NE
                at = (second * 4 + first) * NE
                all_ref[pl.ds(pl.multiple_of(to, NE), NE), :] = source[at : at + NE, :]
    out_ref[:, :] = all_ref[:, :].T


def add_swapped_body(own_hbm, got_hbm, o0, o1, o2, o3, own_ref, got_ref, out_ref, sems):
    outs = (o0, o1, o2, o3)
    order = (2, 1, 3, 0)
    loads = {}
    for g in order:
        span = slice(g * GTOK, (g + 1) * GTOK)
        loads[g] = started(
            [
                pltpu.make_async_copy(own_hbm.at[span], own_ref.at[g], sems.at[3 * g]),
                pltpu.make_async_copy(got_hbm.at[span], got_ref.at[g], sems.at[3 * g + 1]),
            ]
        )
    stores = []
    for g in order:
        for copy in loads[g]:
            copy.wait()
        out_ref[g] = (own_ref[g].astype(F32) + got_ref[g].astype(F32)).astype(BF)
        stores.append(pltpu.make_async_copy(out_ref.at[g], outs[g], sems.at[3 * g + 2]))
        stores[-1].start()
    for copy in stores:
        copy.wait()


def add_second_body(a, b, c, d, *outs):
    for i in range(4):
        span = slice(i * 256, (i + 1) * 256)
        outs[i][:, :] = sum(r[span, :].astype(F32) for r in (a, b, c, d)).astype(BF)


def no_work(values):
    return values


def gather_chip(mine, beside=no_work, values=()):
    pieces = [mine] + [hop(mine, 1, -d) for d in (1, 2, 3)]
    rows = 2 * TOK
    stacked = jnp.concatenate([q[:rows] for q in pieces] + [q[rows:] for q in pieces if q.shape[0] > rows], axis=0)
    if beside is not no_work:
        stacked, values = tie(stacked, values)
    own = [stacked] + [hop(stacked, 2, -d) for d in (2, 1, 3)]
    own = [own[0], own[2], own[1], own[3]]
    oth = [swap(q) for q in own]
    if beside is not no_work:
        oth, values = tie(oth, beside(values))
        return own, oth, values
    return own, oth


def scatter_chip(own, oth, beside=no_work, values=()):
    outs = [shape((GTOK, HALF), BF)] * 4
    block = (GROUPS, GTOK, HALF)
    second = call(
        add_swapped_body,
        outs,
        (own, swap(oth)),
        moved=6 << 20,
        scratch=[pltpu.VMEM(block, BF)] * 3 + [pltpu.SemaphoreType.DMA((12,))],
        anywhere=2,
        outs_anywhere=(0, 1, 2, 3),
    )
    if beside is not no_work:
        second, values = tie(second, values)
    sent = {d: hop(second[d], 2, d) for d in (2, 1, 3)}
    got = [second[0], sent[1], sent[2], sent[3]]
    if beside is not no_work:
        got, values = tie(got, beside(values))
    first = call(add_second_body, [shape((2 * TOK, HALF), BF)] * 4, got, moved=3 << 20)
    sent = {d: hop(first[d], 1, d) for d in (2, 1, 3)}
    terms = [first[0], sent[1], sent[2], sent[3]]
    if beside is not no_work:
        return terms, values
    return terms


def all_dp(block):
    sent = {d: hop_dp(block, -d) for d in (2, 1, 3)}
    return [block, sent[1], sent[2], sent[3]]


def to_dp(parts):
    sent = {d: hop_dp(parts[d], d) for d in (2, 1, 3)}
    return [parts[0], sent[1], sent[2], sent[3]]


def per_device(tokens, picks, halting, w_sel, w_up, w_down, cotangent):
    dp = lax.axis_index("dp")
    place = lax.axis_index("expert")
    core = lax.rem(place, 2)
    sc = jnp.stack([dp, core]).astype(jnp.int32)
    rel = lax.rem(2 * dp + jnp.arange(NE, dtype=jnp.int32), NE) + NE * place
    eid = jnp.broadcast_to(rel.astype(F32)[:, None], (NE, 256))
    sel = w_sel.T[rel]
    sel = jnp.where(core == 0, sel, jnp.concatenate([sel[:, HALF:], sel[:, :HALF]], axis=1))

    def mine_of(array):
        return jnp.where(core == 0, array[:, :HALF], array[:, HALF:])

    def rest_of(array):
        return jnp.where(core == 0, array[:, HALF:], array[:, :HALF])

    def by_core(mine, rest):
        return jnp.where(core == 0, jnp.concatenate([mine, rest], axis=0), jnp.concatenate([rest, mine], axis=0))

    live = halting[None, :, None] > jnp.arange(2, dtype=jnp.int32)[:, None, None]
    named = jnp.where(live, picks, 256).transpose(2, 0, 1).reshape(16, 256).astype(BF)
    rest = swap(jnp.concatenate([rest_of(tokens), named], axis=0))
    state = by_core(mine_of(tokens), rest[:TOK])
    cot = by_core(mine_of(cotangent), swap(rest_of(cotangent)))

    own, oth = gather_chip(jnp.concatenate([state, by_core(named, rest[TOK:])], axis=0))
    v = call(
        routing_body,
        shape((2, GROUPS, NE, GTOK), F32),
        (eid, *own),
        moved=1 << 20,
        scratch=[pltpu.VMEM((GROUPS, 16 * GRP, 256), BF), pltpu.SemaphoreType.DMA((GROUPS,))],
        anywhere=4,
    )

    rows_type = shape((NE, ESLOT, 2 * HALF), BF)
    gather_flops = 2 * 640 * 1024 * 512 * 4 + 2 * 2560 * 512 * 256

    def gather_scratch(w):
        return [
            pltpu.VMEM((GROUPS, GTOK, HALF), BF),
            pltpu.VMEM((GROUPS, GTOK, HALF), BF),
            pltpu.VMEM((NE, ESLOT, 2 * HALF), BF),
            pltpu.VMEM(w.shape, BF),
            pltpu.SemaphoreType.DMA((20,)),
            pltpu.SemaphoreType.DMA,
            pltpu.SemaphoreType.DMA,
        ]

    def project_up(v, own, oth):
        return call(
            up_body,
            [rows_type] + [shape((OWN + EXT, HID), BF)] * 4,
            (sc, v, sel, w_up, *own, *oth),
            flops=gather_flops,
            moved=12 << 20,
            scratch=gather_scratch(w_up),
            smem=1,
            anywhere=9,
            outs_anywhere=(0,),
        )

    def project_cot(v, own, oth):
        return call(
            down_grad_body,
            [rows_type] + [shape((OWN, HID), BF)] * 4,
            (sc, v, w_down, *own, *oth),
            flops=gather_flops,
            moved=12 << 20,
            scratch=gather_scratch(w_down),
            smem=1,
            anywhere=9,
            outs_anywhere=(0,),
        )

    def settle(parts):
        outs = [shape((OWN, HID), BF), shape((OWN, HID), F32), shape((OWN, TOK), F32)]
        return call(settle_body, outs, parts, moved=3 << 20)

    def settle_grad(parts, pre, gate):
        return call(settle_grad_body, shape((OWN + EXT, HID), BF), (*parts, pre, gate), moved=3 << 20)

    def put_of(v):
        return call(put_body, shape((QUADS, QTOK, QSLOT), BF), (v,), flops=4096 * 384 * 256, moved=4 << 20)

    def spread_scratch(w_block, hid_rows):
        return [
            pltpu.VMEM((GROUPS * GTOK, HALF), BF),
            pltpu.VMEM((QUADS, QSLOT, HALF), BF),
            pltpu.VMEM((NE,) + w_block, BF),
            pltpu.VMEM((4, hid_rows, HID), BF),
            pltpu.VMEM((QUADS, QTOK, QSLOT), BF),
            pltpu.SemaphoreType.DMA,
            pltpu.SemaphoreType.DMA((4,)),
            pltpu.SemaphoreType.DMA((QUADS,)),
            pltpu.SemaphoreType.DMA((2 * QUADS,)),
        ]

    y_type = shape((GROUPS * GTOK, HALF), BF)

    def outputs(put, hid, far):
        return call(
            functools.partial(down_body, far),
            y_type,
            (sc, put, w_down, *hid),
            flops=gather_flops // 2,
            moved=8 << 20,
            scratch=spread_scratch((HID, HALF), OWN),
            smem=1,
            anywhere=6,
            outs_anywhere=(0,),
        )

    def grads_in(put, grads, far):
        return call(
            functools.partial(up_grad_body, far),
            y_type,
            (sc, sel, put, w_up, *grads),
            flops=gather_flops // 2,
            moved=8 << 20,
            scratch=spread_scratch((HALF, HID), OWN + EXT),
            smem=1,
            anywhere=6,
            outs_anywhere=(0,),
        )

    def advance(base, terms):
        return (base.astype(F32) + sum(t.astype(F32) for t in terms)).astype(BF)

    x0, *parts = project_up(v[0], own, oth)
    cot, parts = tie(cot, parts)
    cot_own, cot_oth = gather_chip(cot)
    hid0, pre0, gate0 = settle(to_dp(parts))
    put0, put1 = put_of(v[0]), put_of(v[1])
    hid0 = all_dp(hid0)
    c1, *cot_parts = project_cot(v[1], cot_own, cot_oth)
    hid0, cot_parts, put0, put1 = tie(hid0, cot_parts, put0, put1)
    far0 = outputs(put0, hid0, True)
    far0, near_hid = tie(far0, hid0)
    cot_parts = to_dp(cot_parts)
    state1 = advance(state, scatter_chip(outputs(put0, near_hid, False), far0))

    own, oth = gather_chip(state1)
    x1, *parts = project_up(v[1], own, oth)
    hid1, pre1, gate1 = settle(to_dp(parts))
    grad1 = all_dp(settle_grad(cot_parts, pre1, gate1))

    hid1, grad1 = tie(hid1, grad1)
    far1 = grads_in(put1, grad1, True)
    hid1 = all_dp(hid1)
    far1, near_grad1 = tie(far1, grad1)
    cot1 = advance(cot, scatter_chip(grads_in(put1, near_grad1, False), far1))

    def forward_outputs(values):
        put, hid = values
        return outputs(put, hid, True), outputs(put, hid, False)

    cot_own, cot_oth, (out_far, out_near) = gather_chip(cot1, forward_outputs, (put1, hid1))

    c0, *cot_parts = project_cot(v[0], cot_own, cot_oth)
    out_far, out_near, cot_parts = tie(out_far, out_near, cot_parts)
    cot_parts = to_dp(cot_parts)
    state2 = advance(state1, scatter_chip(out_near, out_far))
    grad0 = settle_grad(cot_parts, pre0, gate0)
    c0, grad0 = tie(c0, grad0)
    d_down = call(
        d_down_body,
        shape(w_down.shape, F32),
        (sc, c0, c1, *hid0, *hid1),
        flops=4 * 2560 * 512 * 256,
        moved=16 << 20,
        smem=1,
    )
    grad0 = all_dp(grad0)
    grad0, d_down, state2 = tie(grad0, d_down, state2)
    far0 = grads_in(put0, grad0, True)
    far0, near_grad0 = tie(far0, grad0)
    near0 = grads_in(put0, near_grad0, False)

    def last_work(values):
        grads = values
        d_sel = call(
            d_sel_body, shape((NE, 2 * HALF), F32), (sc, x0, x1, *grads, *grad1), moved=8 << 20, smem=1
        )
        first = jnp.concatenate([d_sel] + [hop(d_sel, 1, -d) for d in (1, 2, 3)], axis=0)
        d_up = call(
            d_up_body,
            shape(w_up.shape, F32),
            (sc, x0, x1, *grads, *grad1),
            flops=4 * 2560 * 512 * 256,
            moved=16 << 20,
            smem=1,
        )
        return first, d_up

    terms, (d_sel, d_up) = scatter_chip(near0, far0, last_work, grad0)
    d_sel = jnp.concatenate([d_sel] + [hop(d_sel, 2, -d) for d in (1, 2, 3)], axis=0)
    d_sel = call(
        d_sel_order_body,
        shape((2 * HALF, EXPERTS), F32),
        (place.reshape(1).astype(jnp.int32), d_sel, swap(d_sel)),
        scratch=[pltpu.VMEM((EXPERTS, 2 * HALF), F32)],
        smem=1,
    )
    cot0 = advance(cot1, terms)

    def whole(array):
        mine = jnp.where(core == 0, array[:TOK], array[TOK:])
        rest = swap(jnp.where(core == 0, array[TOK:], array[:TOK]))
        return jnp.where(
            core == 0, jnp.concatenate([mine, rest], axis=1), jnp.concatenate([rest, mine], axis=1)
        )

    return (whole(state2), whole(cot0), d_up, d_down, d_sel)


def solution(mesh):
    in_specs = (
        P("expert", "dp"),
        P(None, "expert", None),
        P("expert"),
        P("dp", None),
        P("expert", "dp", None),
        P("expert", None, "dp"),
        P("expert", "dp"),
    )
    out_specs = (
        P("expert", "dp"),
        P("expert", "dp"),
        P("expert", "dp", None),
        P("expert", None, "dp"),
        P("dp", None),
    )
    return jax.shard_map(
        per_device, mesh=mesh, in_specs=in_specs, out_specs=out_specs, check_vma=False
    )
```

```python
import functools

import jax
import jax.numpy as jnp
from jax import lax
from jax.experimental import pallas as pl
from jax.experimental.pallas import tpu as pltpu
from jax.sharding import PartitionSpec as P

BF = jnp.bfloat16
F32 = jnp.float32
GELU_C = 0.7978845608028654
GELU_A = 0.044715

TOK = 128
HALF = 256
HID = 256
NE = 8
CAP = 10
GRP = 8
GROUPS = 4
GTOK = GRP * TOK
GSLOT = GRP * CAP
ESLOT = GROUPS * GSLOT
OWN = 2 * ESLOT
EXT = 16
QUADS = 8
QTOK = 4 * TOK
QCAP = 4 * CAP
QSLOT = NE * QCAP
EXPERTS = 256
VMEM = pl.BlockSpec(memory_space=pltpu.VMEM)
HBM = pl.BlockSpec(memory_space=pl.ANY)
SMEM = pl.BlockSpec(memory_space=pltpu.SMEM)


def dev(x, z, c):
    return (x * 4 + z) * 2 + c


PLACES = [(x, z, c) for x in range(4) for z in range(4) for c in range(2)]
SWAP = [(dev(x, z, c), dev(x, z, 1 - c)) for x, z, c in PLACES]


def along(axis, step):
    pairs = []
    for x, z, c in PLACES:
        if (axis + c) % 2 == 1:
            pairs.append((dev(x, z, c), dev((x + step) % 4, z, c)))
        else:
            pairs.append((dev(x, z, c), dev(x, (z + step) % 4, c)))
    return pairs


def hop(value, axis, step):
    return lax.ppermute(value, "expert", along(axis, step % 4))


def swap(value):
    return lax.ppermute(value, "expert", SWAP)


def hop_dp(value, step):
    return lax.ppermute(value, "dp", [(y, (y + step) % 4) for y in range(4)])


def call(body, outs, ins, flops=0, moved=1 << 20, scratch=(), smem=0, anywhere=0, outs_anywhere=(), limit=20):
    flat = [outs] if not isinstance(outs, list) else outs
    specs = [HBM if i in outs_anywhere else VMEM for i in range(len(flat))]
    return pl.pallas_call(
        body,
        out_shape=outs,
        in_specs=[SMEM] * smem + [VMEM] * (len(ins) - smem - anywhere) + [HBM] * anywhere,
        out_specs=specs if isinstance(outs, list) else specs[0],
        scratch_shapes=list(scratch),
        compiler_params=pltpu.CompilerParams(vmem_limit_bytes=limit * 1024 * 1024),
        cost_estimate=pl.CostEstimate(flops=flops, bytes_accessed=moved, transcendentals=0),
    )(*ins)


def shape(dims, dtype):
    return jax.ShapeDtypeStruct(dims, dtype)


def tie(*values):
    return lax.optimization_barrier(values)


def mm(a, b):
    return lax.dot_general(a, b, (((1,), (0,)), ((), ())), preferred_element_type=F32)


def mm_nt(a, b):
    return lax.dot_general(a, b, (((1,), (1,)), ((), ())), preferred_element_type=F32)


def mm_tn(a, b):
    return lax.dot_general(a, b, (((0,), (0,)), ((), ())), preferred_element_type=F32)


def started(copies):
    for copy in copies:
        copy.start()
    return copies


def split_body(sc_ref, tokens_ref, picks_ref, halting_ref, mine_ref, rest_ref):
    first, second = halves(sc_ref)
    mine_ref[:TOK, :] = tokens_ref[:, first]
    rest_ref[:TOK, :] = tokens_ref[:, second]
    for p in range(2):
        named = jnp.where(halting_ref[:, :] > p, picks_ref[p], EXPERTS).astype(F32).astype(BF)
        mine_ref[TOK:, p * TOK : (p + 1) * TOK] = named
        rest_ref[TOK:, p * TOK : (p + 1) * TOK] = named


def join_body(sc_ref, mine_ref, got_ref, out_ref):
    core = sc_ref[1]
    for source, side in ((mine_ref, core), (got_ref, 1 - core)):
        out_ref[pl.ds(pl.multiple_of(side * TOK, TOK), TOK), :] = source[:TOK, :]
        out_ref[pl.ds(pl.multiple_of(2 * TOK + side * 16, 16), 16), :] = source[TOK:, :]


def routing_body(eid_ref, own0, own1, own2, own3, v_ref, named_ref, sems):
    loads = started(
        [
            pltpu.make_async_copy(own.at[GTOK : GTOK + 16 * GRP], named_ref.at[g], sems.at[g])
            for g, own in enumerate((own0, own1, own2, own3))
        ]
    )
    eid = eid_ref[:, :]
    marks = []
    for g in range(GROUPS):
        loads[g].wait()
        for j in range(GRP):
            named = named_ref[g, 16 * j : 16 * j + 16, :].astype(F32)
            mark = jnp.zeros((NE, 256), F32)
            for k in range(16):
                mark = jnp.where(named[k : k + 1, :] == eid, 1.0, mark)
            marks.append(mark)
    before = lax.broadcasted_iota(jnp.int32, (TOK, TOK), 0) < lax.broadcasted_iota(jnp.int32, (TOK, TOK), 1)
    before = jnp.where(before, 1.0, 0.0).astype(BF)
    for p in range(2):
        stacked = jnp.concatenate([m[:, p * TOK : (p + 1) * TOK] for m in marks], axis=0)
        rank = mm(stacked.astype(BF), before)
        for g in range(GROUPS):
            for j in range(GRP):
                at = (g * GRP + j) * NE
                v_ref[p, g, :, j * TOK : (j + 1) * TOK] = jnp.where(
                    stacked[at : at + NE] > 0, rank[at : at + NE] + float(CAP * (j % 4)), -1.0
                )


def put_body(v_ref, put_ref):
    at_lane = lax.broadcasted_iota(jnp.int32, (TOK, QSLOT), 1)
    at_row = lax.broadcasted_iota(jnp.int32, (TOK, QSLOT), 0)
    spread = jnp.where((at_lane >= at_row * QCAP) & (at_lane < (at_row + 1) * QCAP), 1.0, 0.0).astype(BF)
    slot = lax.rem(lax.broadcasted_iota(jnp.int32, (1, QSLOT), 1), QCAP).astype(F32)
    for q in range(QUADS):
        v = v_ref[q // 2, :, (q % 2) * QTOK : (q % 2 + 1) * QTOK]
        turned = jnp.concatenate([v, jnp.zeros((TOK - NE, QTOK), F32)], axis=0).T.astype(BF)
        put_ref[q] = jnp.where(mm(turned, spread) == slot, 1.0, 0.0).astype(BF)


def gather_rows(v_ref, near_of, far_of, x_ref):
    slot = lax.broadcasted_iota(jnp.int32, (QCAP, QTOK), 0).astype(F32)
    for g in range(GROUPS):
        rows = []
        for i in range(2):
            v = v_ref[g, :, i * QTOK : (i + 1) * QTOK]
            pick = jnp.concatenate([jnp.where(slot == v[e : e + 1, :], 1.0, 0.0) for e in range(NE)], axis=0).astype(BF)
            rows.append(
                [
                    mm(pick[:, :256], source(g, 2 * i)) + mm(pick[:, 256:], source(g, 2 * i + 1))
                    for source in (near_of, far_of)
                ]
            )
        for e in range(NE):
            at = slice(e * QCAP, (e + 1) * QCAP)
            for h in range(2):
                x_ref[e, g * GSLOT : (g + 1) * GSLOT, h * HALF : (h + 1) * HALF] = jnp.concatenate(
                    [rows[0][h][at], rows[1][h][at]], axis=0
                ).astype(BF)


def gather_pieces(v_ref, own, oth, x_ref):
    gather_rows(
        v_ref,
        lambda g, d: own[g][d * 256 : (d + 1) * 256, :],
        lambda g, d: oth[d][g * 256 : (g + 1) * 256, :],
        x_ref,
    )


def halves(sc_ref):
    core = sc_ref[1]
    return (
        pl.ds(pl.multiple_of(core * HALF, HALF), HALF),
        pl.ds(pl.multiple_of((1 - core) * HALF, HALF), HALF),
    )


def expert_at(sc_ref, e):
    return lax.rem(2 * sc_ref[0] + e, NE)


def up_body(sc_ref, v_ref, sel_ref, w_up_ref, *refs):
    own, oth, x_ref, parts = refs[0:4], refs[4:8], refs[8], refs[9:13]
    gather_pieces(v_ref, own, oth, x_ref)
    first, second = halves(sc_ref)
    sel = sel_ref[:, :]
    lane_pad = jnp.zeros((1, 192), F32)
    for dy in range(4):
        heads, tails = [], []
        for i in range(2):
            e = 2 * dy + i
            at = expert_at(sc_ref, e)
            rows = x_ref[e]
            total = mm(rows[:, :HALF], w_up_ref[at, first, :]) + mm(rows[:, HALF:], w_up_ref[at, second, :])
            parts[dy][i * ESLOT : (i + 1) * ESLOT, :] = total.astype(BF)
            logit = mm_nt(sel, rows)[e : e + 1, :]
            heads.append(logit[:, :256])
            tails.append(jnp.concatenate([logit[:, 256:], lane_pad], axis=1))
        logits = jnp.concatenate(heads + tails, axis=0)
        high = logits.astype(BF).astype(F32)
        low = logits - high
        parts[dy][OWN:, :] = jnp.concatenate([high, low, jnp.zeros((8, 256), F32)], axis=0).astype(BF)


def down_grad_body(sc_ref, v_ref, w_down_ref, *refs):
    own, oth, x_ref, parts = refs[0:4], refs[4:8], refs[8], refs[9:13]
    gather_pieces(v_ref, own, oth, x_ref)
    first, second = halves(sc_ref)
    for e in range(NE):
        at = expert_at(sc_ref, e)
        rows = x_ref[e]
        total = mm_nt(rows[:, :HALF], w_down_ref[at, :, first]) + mm_nt(rows[:, HALF:], w_down_ref[at, :, second])
        parts[e // 2][(e % 2) * ESLOT : (e % 2 + 1) * ESLOT, :] = total.astype(BF)


def as_columns(rows):
    turned = jnp.concatenate([rows, jnp.zeros((TOK - rows.shape[0], 256), F32)], axis=0).T
    return jnp.concatenate([turned[:, 0:1], turned[:64, 2:3], turned[:, 1:2], turned[:64, 3:4]], axis=0)


def as_rows(column):
    wide = jnp.broadcast_to(column, (OWN, TOK))
    lane = lax.broadcasted_iota(jnp.int32, (256, TOK), 1)
    pad = jnp.zeros((192, TOK), F32)
    pieces = (
        wide[0:256],
        wide[ESLOT : ESLOT + 256],
        jnp.concatenate([wide[256:ESLOT], pad], axis=0),
        jnp.concatenate([wide[ESLOT + 256 :], pad], axis=0),
    )
    mixed = jnp.zeros((256, TOK), F32)
    for i, piece in enumerate(pieces):
        mixed = jnp.where(lane == i, piece, mixed)
    return mixed.T[:EXT]


def settle_body(p0, p1, p2, p3, hid_ref, pre_ref, gate_ref):
    def total(lo, hi):
        return sum(p[lo:hi, :].astype(F32) for p in (p0, p1, p2, p3))

    extra = total(OWN, OWN + EXT)
    gate = jax.nn.sigmoid(as_columns(extra[0:4] + extra[4:8]))
    pre = total(0, OWN)
    pre_ref[:, :] = pre
    gate_ref[:, :] = jnp.broadcast_to(gate, (OWN, TOK))
    inner = GELU_C * (pre + GELU_A * pre * pre * pre)
    hid_ref[:, :] = (gate * (0.5 * pre * (1.0 + jnp.tanh(inner)))).astype(BF)


def settle_grad_body(*refs):
    parts, (pre_ref, gate_ref, grad_ref) = refs[:-3], refs[-3:]
    total = sum(p[:, :].astype(F32) for p in parts)
    pre = pre_ref[:, :]
    gate = gate_ref[:, 0:1]
    tangent = jnp.tanh(GELU_C * (pre + GELU_A * pre * pre * pre))
    hidden = (0.5 * pre * (1.0 + tangent)).astype(BF).astype(F32)
    slope = 0.5 * (1.0 + tangent) + 0.5 * pre * (1.0 - tangent * tangent) * GELU_C * (1.0 + 3.0 * GELU_A * pre * pre)
    score = jnp.sum(hidden * total, axis=1, keepdims=True)
    grad_ref[0:OWN, :] = (gate * total * slope).astype(BF)
    grad_ref[OWN:, :] = as_rows(score * gate * (1.0 - gate)).astype(BF)


def place_rows(out_ref, e, pair):
    for q in range(QUADS):
        span = slice(q * QCAP, (q + 1) * QCAP)
        out_ref[q, e * QCAP : (e + 2) * QCAP, :] = jnp.concatenate([pair[0][span], pair[1][span]], axis=0).astype(BF)


def scatter_rows(far, put_ref, out_ref, y_ref):
    for q in range(QUADS):
        rows = mm(put_ref[q], out_ref[q]).astype(BF)
        g, i = q // 2, q % 2
        for k in range(2):
            at = ((2 * i + k) * 4 + g if far else 2 * q + k) * 256
            y_ref[at : at + 256, :] = rows[k * 256 : (k + 1) * 256]


def down_body(far, sc_ref, put_ref, w_down_ref, h0, h1, h2, h3, y_ref, out_ref):
    hid = (h0, h1, h2, h3)
    cols = halves(sc_ref)[int(far)]
    for d in range(4):
        pair = [
            mm(hid[d][i * ESLOT : (i + 1) * ESLOT, :], w_down_ref[expert_at(sc_ref, 2 * d + i), :, cols])
            for i in range(2)
        ]
        place_rows(out_ref, 2 * d, pair)
    scatter_rows(far, put_ref, out_ref, y_ref)


def logit_rows(extras):
    rows = []
    for extra in extras:
        extra = extra.astype(F32)
        for i in range(2):
            rows.append(jnp.concatenate([extra[i : i + 1, :], extra[2 + i : 3 + i, :64]], axis=1))
    return jnp.concatenate(rows, axis=0)


def up_grad_body(far, sc_ref, sel_ref, put_ref, w_up_ref, h0, h1, h2, h3, y_ref, out_ref):
    grads = (h0, h1, h2, h3)
    part = slice(HALF, 2 * HALF) if far else slice(0, HALF)
    cols = halves(sc_ref)[int(far)]
    sel = sel_ref[:, part].astype(F32)
    rows = logit_rows([g[OWN:, :] for g in grads])
    rows = jnp.concatenate([rows, jnp.zeros((NE, 64), F32)], axis=1)
    columns = jnp.concatenate([rows, jnp.zeros((TOK - NE, 384), F32)], axis=0).T
    for d in range(4):
        pair = []
        for i in range(2):
            e = 2 * d + i
            out = mm_nt(grads[d][i * ESLOT : (i + 1) * ESLOT, :], w_up_ref[expert_at(sc_ref, e), cols, :])
            pair.append(out + columns[:ESLOT, e : e + 1] * sel[e : e + 1, :])
        place_rows(out_ref, 2 * d, pair)
    scatter_rows(far, put_ref, out_ref, y_ref)


def d_down_body(sc_ref, c0_ref, c1_ref, *refs):
    hid, d_ref = (refs[0:4], refs[4:8]), refs[8]
    first, second = halves(sc_ref)
    for e in range(NE):
        at = expert_at(sc_ref, e)
        span = slice((e % 2) * ESLOT, (e % 2 + 1) * ESLOT)
        for h, cols in enumerate((first, second)):
            part = slice(h * HALF, (h + 1) * HALF)
            d_ref[at, :, cols] = mm_tn(hid[0][e // 2][span, :], c0_ref[e, :, part]) + mm_tn(
                hid[1][e // 2][span, :], c1_ref[e, :, part]
            )


def d_up_body(sc_ref, x0_ref, x1_ref, *refs):
    grads, d_ref = (refs[0:4], refs[4:8]), refs[8]
    first, second = halves(sc_ref)
    for e in range(NE):
        at = expert_at(sc_ref, e)
        span = slice((e % 2) * ESLOT, (e % 2 + 1) * ESLOT)
        for h, cols in enumerate((first, second)):
            part = slice(h * HALF, (h + 1) * HALF)
            d_ref[at, cols, :] = mm_tn(x0_ref[e, :, part], grads[0][e // 2][span, :]) + mm_tn(
                x1_ref[e, :, part], grads[1][e // 2][span, :]
            )


def d_sel_body(sc_ref, x0_ref, x1_ref, *refs):
    grads, code_ref, sel_ref = (refs[0:4], refs[4:8]), refs[8], refs[9]
    first, second = halves(sc_ref)
    rows = [logit_rows([g[OWN:, :] for g in grads[p]]).astype(BF) for p in range(2)]
    for e in range(NE):
        at = expert_at(sc_ref, e)
        d_sel = (mm(rows[0], x0_ref[e]) + mm(rows[1], x1_ref[e]))[e : e + 1, :]
        sel_ref[pl.ds(at, 1), first] = d_sel[:, :HALF]
        sel_ref[pl.ds(at, 1), second] = d_sel[:, HALF:]
    value = jnp.concatenate([sel_ref[:, :HALF], sel_ref[:, HALF:]], axis=0)
    high = value.astype(BF)
    code_ref[: 2 * NE, :] = high
    code_ref[2 * NE :, :] = (value - high.astype(F32)).astype(BF)


def last_sum_body(sc_ref, cot_ref, state_ref, t0, t1, t2, t3, mine_ref, rest_ref):
    core = sc_ref[1]
    terms = (t0, t1, t2, t3)
    for out_ref, side in ((mine_ref, core), (rest_ref, 1 - core)):
        for k, base_ref in enumerate((cot_ref, state_ref)):
            total = base_ref[pl.ds(pl.multiple_of(side * TOK, TOK), TOK), :].astype(F32)
            for term in terms:
                total = total + term[pl.ds(pl.multiple_of((2 * k + side) * TOK, TOK), TOK), :].astype(F32)
            out_ref[k * TOK : (k + 1) * TOK, :] = total.astype(BF)
    for d in range(4):
        rest_ref[(2 + d) * TOK : (3 + d) * TOK, :] = terms[(4 - d) % 4][4 * TOK :, :]


def last_order_body(sc_ref, mine_ref, own_ref, got_ref, cot_ref, state_ref, d_sel_ref, all_ref):
    core = sc_ref[1]
    first, second = halves(sc_ref)
    for k, out_ref in enumerate((cot_ref, state_ref)):
        out_ref[:, first] = mine_ref[k * TOK : (k + 1) * TOK, :]
        out_ref[:, second] = got_ref[k * TOK : (k + 1) * TOK, :]
    for source, side in ((own_ref, core), (got_ref, 1 - core)):
        for d1 in range(4):
            for d2 in range(4):
                x = lax.rem(sc_ref[2] + jnp.where(side == 0, d1, d2), 4)
                z = lax.rem(sc_ref[3] + jnp.where(side == 0, d2, d1), 4)
                to = pl.ds(pl.multiple_of(((x * 4 + z) * 2 + side) * NE, NE), NE)
                at = 2 * TOK + (d1 * 4 + d2) * 32
                block = source[at : at + 32, :].astype(F32)
                value = block[: 2 * NE] + block[2 * NE :]
                all_ref[to, :HALF] = value[:NE]
                all_ref[to, HALF:] = value[NE:]
    d_sel_ref[:, :] = all_ref[:, :].T


def add_swapped_body(own_ref, got_ref, *outs):
    for g in range(GROUPS):
        span = slice(g * GTOK, (g + 1) * GTOK)
        outs[g][:, :] = (own_ref[span, :].astype(F32) + got_ref[span, :].astype(F32)).astype(BF)


def add_second_body(count, *refs):
    outs = refs[-4:]
    for k in range(count):
        for i in range(4):
            span = slice(i * 256, (i + 1) * 256)
            total = sum(r[span, :].astype(F32) for r in refs[4 * k : 4 * k + 4])
            outs[i][k * 256 : (k + 1) * 256, :] = total.astype(BF)
    for k, rider in enumerate(refs[4 * count : -4]):
        for out in outs:
            out[256 * count + 32 * k : 256 * count + 32 * (k + 1), :] = rider[:, :]


def gather_second(stacked):
    own = {d: hop(stacked, 2, -d) for d in (2, 1, 3)}
    return [stacked, own[1], own[2], own[3]]


def gather_first(mine):
    return jnp.concatenate([mine] + [hop(mine, 1, -d) for d in (1, 2, 3)], axis=0)


def scatter_first(own, oth):
    outs = [shape((GTOK, HALF), BF)] * 4
    return call(add_swapped_body, outs, (own, swap(oth)), moved=6 << 20)


def scatter_second(second):
    sent = {d: hop(second[d], 2, d) for d in (2, 1, 3)}
    return [second[0], sent[1], sent[2], sent[3]]


def add_second(*sums, riders=()):
    outs = [shape((2 * TOK * len(sums) + 32 * len(riders), HALF), BF)] * 4
    body = functools.partial(add_second_body, len(sums))
    return call(body, outs, (*sum(sums, []), *riders), moved=3 << 20)


def scatter_third(first):
    sent = {d: hop(first[d], 1, d) for d in (2, 1, 3)}
    return [first[0], sent[1], sent[2], sent[3]]


def all_dp(block):
    sent = {d: hop_dp(block, -d) for d in (2, 1, 3)}
    return [block, sent[1], sent[2], sent[3]]


def to_dp(parts):
    sent = {d: hop_dp(parts[d], d) for d in (2, 1, 3)}
    return [parts[0], sent[1], sent[2], sent[3]]


def per_device(tokens, picks, halting, w_sel, w_up, w_down, cotangent):
    dp = lax.axis_index("dp")
    place = lax.axis_index("expert")
    core = lax.rem(place, 2)
    sc = jnp.stack([dp, core, place // 8, lax.rem(place // 2, 4)]).astype(jnp.int32)
    rel = lax.rem(2 * dp + jnp.arange(NE, dtype=jnp.int32), NE) + NE * place
    eid = jnp.broadcast_to(rel.astype(F32)[:, None], (NE, 256))
    sel = w_sel.T[rel]
    sel = jnp.where(core == 0, sel, jnp.concatenate([sel[:, HALF:], sel[:, :HALF]], axis=1))

    block = shape((TOK + 16, HALF), BF)
    mine, rest = call(split_body, [block] * 2, (sc, tokens, picks.transpose(0, 2, 1), halting.reshape(1, TOK)), smem=1, limit=60)
    joined = call(join_body, shape((2 * TOK + 32, HALF), BF), (sc, mine, swap(rest)), smem=1)
    state = joined[: 2 * TOK]
    pieces = [joined] + [hop(joined, 1, -d) for d in (1, 2, 3)]
    stacked = jnp.concatenate([q[: 2 * TOK] for q in pieces] + [q[2 * TOK :] for q in pieces], axis=0)
    stacked, cotangent = tie(stacked, cotangent)
    own = gather_second(stacked)
    mine = lax.dynamic_slice_in_dim(cotangent, core * HALF, HALF, 1)
    rest = swap(lax.dynamic_slice_in_dim(cotangent, (1 - core) * HALF, HALF, 1))
    cot = jnp.where(core == 0, jnp.concatenate([mine, rest], axis=0), jnp.concatenate([rest, mine], axis=0))
    cot_stacked = gather_first(cot)
    own[2], cot_stacked = tie(own[2], cot_stacked)
    oth = [swap(q) for q in own]
    v = call(
        routing_body,
        shape((2, GROUPS, NE, GTOK), F32),
        (eid, *own),
        moved=1 << 20,
        scratch=[pltpu.VMEM((GROUPS, 16 * GRP, 256), BF), pltpu.SemaphoreType.DMA((GROUPS,))],
        anywhere=4,
    )

    rows_type = shape((NE, ESLOT, 2 * HALF), BF)
    gather_flops = 2 * 640 * 1024 * 512 * 4 + 2 * 2560 * 512 * 256

    def project_up(v, own, oth):
        return call(
            up_body,
            [rows_type] + [shape((OWN + EXT, HID), BF)] * 4,
            (sc, v, sel, w_up, *own, *oth),
            flops=gather_flops,
            moved=12 << 20,
            smem=1,
        )

    def project_cot(v, own, oth):
        return call(
            down_grad_body,
            [rows_type] + [shape((OWN, HID), BF)] * 4,
            (sc, v, w_down, *own, *oth),
            flops=gather_flops,
            moved=12 << 20,
            smem=1,
        )

    def settle(parts):
        outs = [shape((OWN, HID), BF), shape((OWN, HID), F32), shape((OWN, TOK), F32)]
        return call(settle_body, outs, parts, moved=3 << 20)

    def settle_grad(parts, pre, gate):
        return call(settle_grad_body, shape((OWN + EXT, HID), BF), (*parts, pre, gate), moved=3 << 20)

    def put_of(v):
        return call(put_body, shape((QUADS, QTOK, QSLOT), BF), (v,), flops=4096 * 384 * 256, moved=4 << 20)

    y_type = shape((GROUPS * GTOK, HALF), BF)
    out_scratch = [pltpu.VMEM((QUADS, QSLOT, HALF), BF)]

    def both(body, ins, last):
        def half(far, last):
            return call(
                functools.partial(body, far),
                y_type,
                (*ins, *last),
                flops=gather_flops // 2,
                moved=8 << 20,
                scratch=out_scratch,
                smem=1,
            )

        far = half(True, last)
        far, last = tie(far, last)
        return half(False, last), far

    def outputs(put, hid):
        return both(down_body, (sc, put, w_down), hid)

    def grads_in(put, grads):
        return both(up_grad_body, (sc, sel, put, w_up), grads)

    def advance(base, terms):
        return (base.astype(F32) + sum(t.astype(F32) for t in terms)).astype(BF)

    x0, *parts = project_up(v[0], own, oth)
    parts, cot_stacked = tie(parts, cot_stacked)
    parts = to_dp(parts)
    cot_own = {0: cot_stacked, 2: hop(cot_stacked, 2, -2)}
    parts, cot_own[2] = tie(parts, cot_own[2])
    hid0, pre0, gate0 = settle(parts)
    put0, put1 = put_of(v[0]), put_of(v[1])
    hid0, cot_stacked = tie(hid0, cot_stacked)
    hid0 = all_dp(hid0)
    cot_own[1], cot_own[3] = hop(cot_stacked, 2, -1), hop(cot_stacked, 2, -3)
    hid0, put0, put1, cot_own = tie(hid0, put0, put1, cot_own)
    second = scatter_first(*outputs(put0, hid0))
    second, cot_own = tie(second, cot_own)
    got = scatter_second(second)
    cot_own = [cot_own[d] for d in range(4)]
    c1, *cot_parts = project_cot(v[1], cot_own, [swap(q) for q in cot_own])
    got, cot_parts = tie(got, cot_parts)
    state1 = advance(state, scatter_third(add_second(got)))

    stacked = gather_first(state1)
    stacked, cot_parts = tie(stacked, cot_parts)
    own = gather_second(stacked)
    cot_parts = to_dp(cot_parts)
    own[2], cot_parts = tie(own[2], cot_parts)
    x1, *parts = project_up(v[1], own, [swap(q) for q in own])
    hid1, pre1, gate1 = settle(to_dp(parts))
    grad1 = all_dp(settle_grad(cot_parts, pre1, gate1))

    hid1, grad1 = tie(hid1, grad1)
    second = scatter_first(*grads_in(put1, grad1))
    second, hid1 = tie(second, hid1)
    got = scatter_second(second)
    hid1 = {0: hid1, 2: hop_dp(hid1, -2)}
    got, hid1 = tie(got, hid1)
    cot1 = advance(cot, scatter_third(add_second(got)))
    stacked = gather_first(cot1)
    stacked, hid1[0] = tie(stacked, hid1[0])
    own = gather_second(stacked)
    hid1[1], hid1[3] = hop_dp(hid1[0], -1), hop_dp(hid1[0], -3)
    own[2], hid1 = tie(own[2], hid1)
    hid1 = [hid1[d] for d in range(4)]

    c0, *cot_parts = project_cot(v[0], own, [swap(q) for q in own])
    cot_parts, hid1 = tie(cot_parts, hid1)
    cot_parts = to_dp(cot_parts)
    second = scatter_first(*outputs(put1, hid1))
    cot_parts, second = tie(cot_parts, second)
    grad0 = settle_grad(cot_parts, pre0, gate0)
    grad0, second, c0 = tie(grad0, second, c0)
    state_got = scatter_second(second)
    grad0 = all_dp(grad0)
    d_down = call(
        d_down_body,
        shape(w_down.shape, F32),
        (sc, c0, c1, *hid0, *hid1),
        flops=4 * 2560 * 512 * 256,
        moved=16 << 20,
        smem=1,
    )
    grad0, d_down = tie(grad0, d_down)
    near, far = grads_in(put0, grad0)
    near, state_got = tie(near, state_got)
    second = scatter_first(near, far)
    second, grad0 = tie(second, grad0)
    got = scatter_second(second)
    d_sel = call(
        d_sel_body,
        shape((4 * NE, HALF), BF),
        (sc, x0, x1, *grad0, *grad1),
        moved=8 << 20,
        scratch=[pltpu.VMEM((NE, 2 * HALF), F32)],
        smem=1,
    )
    riders = [d_sel] + [hop(d_sel, 2, -d) for d in (1, 2, 3)]
    d_up = call(
        d_up_body,
        shape(w_up.shape, F32),
        (sc, x0, x1, *grad0, *grad1),
        flops=4 * 2560 * 512 * 256,
        moved=16 << 20,
        smem=1,
    )
    got, riders, d_up = tie(got, riders, d_up)
    terms = scatter_third(add_second(got, state_got, riders=riders))
    mine, rest = call(
        last_sum_body,
        [shape((2 * TOK, HALF), BF), shape((6 * TOK, HALF), BF)],
        (sc, cot1, state1, *terms),
        smem=1,
    )
    d_tokens, layer_out, d_sel = call(
        last_order_body,
        [shape((TOK, 2 * HALF), BF)] * 2 + [shape((2 * HALF, EXPERTS), F32)],
        (sc, mine, rest, swap(rest)),
        scratch=[pltpu.VMEM((EXPERTS, 2 * HALF), F32)],
        smem=1,
    )
    return (layer_out, d_tokens, d_up, d_down, d_sel)


def solution(mesh):
    in_specs = (
        P("expert", "dp"),
        P(None, "expert", None),
        P("expert"),
        P("dp", None),
        P("expert", "dp", None),
        P("expert", None, "dp"),
        P("expert", "dp"),
    )
    out_specs = (
        P("expert", "dp"),
        P("expert", "dp"),
        P("expert", "dp", None),
        P("expert", None, "dp"),
        P("dp", None),
    )
    return jax.shard_map(
        per_device, mesh=mesh, in_specs=in_specs, out_specs=out_specs, check_vma=False
    )
```

```python
import functools

import jax
import jax.numpy as jnp
from jax import lax
from jax.experimental import pallas as pl
from jax.experimental.pallas import tpu as pltpu
from jax.sharding import PartitionSpec as P

BF = jnp.bfloat16
F32 = jnp.float32
GELU_C = 0.7978845608028654
GELU_A = 0.044715

TOK = 128
HALF = 256
HID = 256
NE = 8
CAP = 10
GRP = 8
GROUPS = 4
GTOK = GRP * TOK
GSLOT = GRP * CAP
ESLOT = GROUPS * GSLOT
OWN = 2 * ESLOT
EXT = 16
QUADS = 8
QTOK = 4 * TOK
QCAP = 4 * CAP
QSLOT = NE * QCAP
EXPERTS = 256
PIECE = 2 * TOK + 32
ORDER = (2, 1, 3)
VMEM = pl.BlockSpec(memory_space=pltpu.VMEM)
HBM = pl.BlockSpec(memory_space=pl.ANY)
SMEM = pl.BlockSpec(memory_space=pltpu.SMEM)


def dev(x, z, c):
    return (x * 4 + z) * 2 + c


PLACES = [(x, z, c) for x in range(4) for z in range(4) for c in range(2)]
SWAP = [(dev(x, z, c), dev(x, z, 1 - c)) for x, z, c in PLACES]


def along(axis, step):
    pairs = []
    for x, z, c in PLACES:
        if (axis + c) % 2 == 1:
            pairs.append((dev(x, z, c), dev((x + step) % 4, z, c)))
        else:
            pairs.append((dev(x, z, c), dev(x, (z + step) % 4, c)))
    return pairs


def hop(value, axis, step):
    return lax.ppermute(value, "expert", along(axis, step % 4))


def swap(value):
    return lax.ppermute(value, "expert", SWAP)


def hop_dp(value, step):
    return lax.ppermute(value, "dp", [(y, (y + step) % 4) for y in range(4)])


def call(body, outs, ins, flops=0, moved=1 << 20, scratch=(), smem=0, anywhere=0, outs_anywhere=(), limit=20):
    flat = [outs] if not isinstance(outs, list) else outs
    specs = [HBM if i in outs_anywhere else VMEM for i in range(len(flat))]
    return pl.pallas_call(
        body,
        out_shape=outs,
        in_specs=[SMEM] * smem + [VMEM] * (len(ins) - smem - anywhere) + [HBM] * anywhere,
        out_specs=specs if isinstance(outs, list) else specs[0],
        scratch_shapes=list(scratch),
        compiler_params=pltpu.CompilerParams(vmem_limit_bytes=limit * 1024 * 1024),
        cost_estimate=pl.CostEstimate(flops=flops, bytes_accessed=moved, transcendentals=0),
    )(*ins)


def shape(dims, dtype):
    return jax.ShapeDtypeStruct(dims, dtype)


def tie(*values):
    return lax.optimization_barrier(values)


def mm(a, b):
    return lax.dot_general(a, b, (((1,), (0,)), ((), ())), preferred_element_type=F32)


def mm_nt(a, b):
    return lax.dot_general(a, b, (((1,), (1,)), ((), ())), preferred_element_type=F32)


def mm_tn(a, b):
    return lax.dot_general(a, b, (((0,), (0,)), ((), ())), preferred_element_type=F32)


def routing_body(eid_ref, own0, own1, own2, own3, v_ref):
    own = (own0, own1, own2, own3)
    eid = eid_ref[:, :]
    marks = []
    for g in range(GROUPS):
        for j in range(GRP):
            at = j // 2 * PIECE + 2 * TOK + j % 2 * 16
            named = own[g][at : at + 16, :].astype(F32)
            mark = jnp.zeros((NE, 256), F32)
            for k in range(16):
                mark = jnp.where(named[k : k + 1, :] == eid, 1.0, mark)
            marks.append(mark)
    before = lax.broadcasted_iota(jnp.int32, (TOK, TOK), 0) < lax.broadcasted_iota(jnp.int32, (TOK, TOK), 1)
    before = jnp.where(before, 1.0, 0.0).astype(BF)
    for p in range(2):
        stacked = jnp.concatenate([m[:, p * TOK : (p + 1) * TOK] for m in marks], axis=0)
        rank = mm(stacked.astype(BF), before)
        for g in range(GROUPS):
            for j in range(GRP):
                at = (g * GRP + j) * NE
                v_ref[p, g, :, j * TOK : (j + 1) * TOK] = jnp.where(
                    stacked[at : at + NE] > 0, rank[at : at + NE] + float(CAP * (j % 4)), -1.0
                )


def put_body(v_ref, put_ref):
    at_lane = lax.broadcasted_iota(jnp.int32, (TOK, QSLOT), 1)
    at_row = lax.broadcasted_iota(jnp.int32, (TOK, QSLOT), 0)
    spread = jnp.where((at_lane >= at_row * QCAP) & (at_lane < (at_row + 1) * QCAP), 1.0, 0.0).astype(BF)
    slot = lax.rem(lax.broadcasted_iota(jnp.int32, (1, QSLOT), 1), QCAP).astype(F32)
    for q in range(QUADS):
        v = v_ref[q // 2, :, (q % 2) * QTOK : (q % 2 + 1) * QTOK]
        turned = jnp.concatenate([v, jnp.zeros((TOK - NE, QTOK), F32)], axis=0).T.astype(BF)
        put_ref[q] = jnp.where(mm(turned, spread) == slot, 1.0, 0.0).astype(BF)


def gather_rows(v_ref, near_of, far_of, x_ref):
    slot = lax.broadcasted_iota(jnp.int32, (QCAP, QTOK), 0).astype(F32)
    for g in range(GROUPS):
        rows = []
        for i in range(2):
            v = v_ref[g, :, i * QTOK : (i + 1) * QTOK]
            pick = jnp.concatenate([jnp.where(slot == v[e : e + 1, :], 1.0, 0.0) for e in range(NE)], axis=0).astype(BF)
            rows.append(
                [
                    mm(pick[:, :256], source(g, 2 * i)) + mm(pick[:, 256:], source(g, 2 * i + 1))
                    for source in (near_of, far_of)
                ]
            )
        for e in range(NE):
            at = slice(e * QCAP, (e + 1) * QCAP)
            for h in range(2):
                x_ref[e, g * GSLOT : (g + 1) * GSLOT, h * HALF : (h + 1) * HALF] = jnp.concatenate(
                    [rows[0][h][at], rows[1][h][at]], axis=0
                ).astype(BF)


def gather_pieces(v_ref, own, oth, x_ref):
    step = own[0].shape[0] // 4
    gather_rows(
        v_ref,
        lambda g, d: own[g][d * step : d * step + 256, :],
        lambda g, d: oth[d][g * step : g * step + 256, :],
        x_ref,
    )


def halves(sc_ref):
    core = sc_ref[1]
    return (
        pl.ds(pl.multiple_of(core * HALF, HALF), HALF),
        pl.ds(pl.multiple_of((1 - core) * HALF, HALF), HALF),
    )


def expert_at(sc_ref, e):
    return lax.rem(2 * sc_ref[0] + e, NE)


def up_body(sc_ref, v_ref, sel_ref, w_up_ref, *refs):
    own, oth, x_ref, parts = refs[0:4], refs[4:8], refs[8], refs[9:13]
    gather_pieces(v_ref, own, oth, x_ref)
    first, second = halves(sc_ref)
    sel = sel_ref[:, :]
    lane_pad = jnp.zeros((1, 192), F32)
    for dy in range(4):
        heads, tails = [], []
        for i in range(2):
            e = 2 * dy + i
            at = expert_at(sc_ref, e)
            rows = x_ref[e]
            total = mm(rows[:, :HALF], w_up_ref[at, first, :]) + mm(rows[:, HALF:], w_up_ref[at, second, :])
            parts[dy][i * ESLOT : (i + 1) * ESLOT, :] = total.astype(BF)
            logit = mm_nt(sel, rows)[e : e + 1, :]
            heads.append(logit[:, :256])
            tails.append(jnp.concatenate([logit[:, 256:], lane_pad], axis=1))
        logits = jnp.concatenate(heads + tails, axis=0)
        high = logits.astype(BF).astype(F32)
        low = logits - high
        parts[dy][OWN:, :] = jnp.concatenate([high, low, jnp.zeros((8, 256), F32)], axis=0).astype(BF)


def down_grad_body(sc_ref, v_ref, w_down_ref, *refs):
    own, oth, x_ref, parts = refs[0:4], refs[4:8], refs[8], refs[9:13]
    gather_pieces(v_ref, own, oth, x_ref)
    first, second = halves(sc_ref)
    for e in range(NE):
        at = expert_at(sc_ref, e)
        rows = x_ref[e]
        total = mm_nt(rows[:, :HALF], w_down_ref[at, :, first]) + mm_nt(rows[:, HALF:], w_down_ref[at, :, second])
        parts[e // 2][(e % 2) * ESLOT : (e % 2 + 1) * ESLOT, :] = total.astype(BF)


def as_columns(rows):
    turned = jnp.concatenate([rows, jnp.zeros((TOK - rows.shape[0], 256), F32)], axis=0).T
    return jnp.concatenate([turned[:, 0:1], turned[:64, 2:3], turned[:, 1:2], turned[:64, 3:4]], axis=0)


def as_rows(column):
    wide = jnp.broadcast_to(column, (OWN, TOK))
    lane = lax.broadcasted_iota(jnp.int32, (256, TOK), 1)
    pad = jnp.zeros((192, TOK), F32)
    pieces = (
        wide[0:256],
        wide[ESLOT : ESLOT + 256],
        jnp.concatenate([wide[256:ESLOT], pad], axis=0),
        jnp.concatenate([wide[ESLOT + 256 :], pad], axis=0),
    )
    mixed = jnp.zeros((256, TOK), F32)
    for i, piece in enumerate(pieces):
        mixed = jnp.where(lane == i, piece, mixed)
    return mixed.T[:EXT]


def settle_body(p0, p1, p2, p3, hid_ref, pre_ref, gate_ref):
    def total(lo, hi):
        return sum(p[lo:hi, :].astype(F32) for p in (p0, p1, p2, p3))

    extra = total(OWN, OWN + EXT)
    gate = jax.nn.sigmoid(as_columns(extra[0:4] + extra[4:8]))
    pre = total(0, OWN)
    pre_ref[:, :] = pre
    gate_ref[:, :] = jnp.broadcast_to(gate, (OWN, TOK))
    inner = GELU_C * (pre + GELU_A * pre * pre * pre)
    hid_ref[:, :] = (gate * (0.5 * pre * (1.0 + jnp.tanh(inner)))).astype(BF)


def settle_grad_body(*refs):
    parts, (pre_ref, gate_ref, grad_ref) = refs[:-3], refs[-3:]
    total = sum(p[:, :].astype(F32) for p in parts)
    pre = pre_ref[:, :]
    gate = gate_ref[:, 0:1]
    tangent = jnp.tanh(GELU_C * (pre + GELU_A * pre * pre * pre))
    hidden = (0.5 * pre * (1.0 + tangent)).astype(BF).astype(F32)
    slope = 0.5 * (1.0 + tangent) + 0.5 * pre * (1.0 - tangent * tangent) * GELU_C * (1.0 + 3.0 * GELU_A * pre * pre)
    score = jnp.sum(hidden * total, axis=1, keepdims=True)
    grad_ref[0:OWN, :] = (gate * total * slope).astype(BF)
    grad_ref[OWN:, :] = as_rows(score * gate * (1.0 - gate)).astype(BF)


def place_rows(out_ref, e, pair):
    for q in range(QUADS):
        span = slice(q * QCAP, (q + 1) * QCAP)
        out_ref[q, e * QCAP : (e + 2) * QCAP, :] = jnp.concatenate([pair[0][span], pair[1][span]], axis=0).astype(BF)


def scatter_rows(far, put_ref, out_ref, y_ref):
    for q in range(QUADS):
        rows = mm(put_ref[q], out_ref[q]).astype(BF)
        g, i = q // 2, q % 2
        for k in range(2):
            at = ((2 * i + k) * 4 + g if far else 2 * q + k) * 256
            y_ref[at : at + 256, :] = rows[k * 256 : (k + 1) * 256]


def down_body(far, sc_ref, put_ref, w_down_ref, h0, h1, h2, h3, y_ref, out_ref):
    hid = (h0, h1, h2, h3)
    cols = halves(sc_ref)[int(far)]
    for d in range(4):
        pair = [
            mm(hid[d][i * ESLOT : (i + 1) * ESLOT, :], w_down_ref[expert_at(sc_ref, 2 * d + i), :, cols])
            for i in range(2)
        ]
        place_rows(out_ref, 2 * d, pair)
    scatter_rows(far, put_ref, out_ref, y_ref)


def logit_rows(extras):
    rows = []
    for extra in extras:
        extra = extra.astype(F32)
        for i in range(2):
            rows.append(jnp.concatenate([extra[i : i + 1, :], extra[2 + i : 3 + i, :64]], axis=1))
    return jnp.concatenate(rows, axis=0)


def up_grad_body(far, sc_ref, sel_ref, put_ref, w_up_ref, h0, h1, h2, h3, y_ref, out_ref):
    grads = (h0, h1, h2, h3)
    part = slice(HALF, 2 * HALF) if far else slice(0, HALF)
    cols = halves(sc_ref)[int(far)]
    sel = sel_ref[:, part].astype(F32)
    rows = logit_rows([g[OWN:, :] for g in grads])
    rows = jnp.concatenate([rows, jnp.zeros((NE, 64), F32)], axis=1)
    columns = jnp.concatenate([rows, jnp.zeros((TOK - NE, 384), F32)], axis=0).T
    for d in range(4):
        pair = []
        for i in range(2):
            e = 2 * d + i
            out = mm_nt(grads[d][i * ESLOT : (i + 1) * ESLOT, :], w_up_ref[expert_at(sc_ref, e), cols, :])
            pair.append(out + columns[:ESLOT, e : e + 1] * sel[e : e + 1, :])
        place_rows(out_ref, 2 * d, pair)
    scatter_rows(far, put_ref, out_ref, y_ref)


def d_down_body(sc_ref, c0_ref, c1_ref, *refs):
    hid, d_ref = (refs[0:4], refs[4:8]), refs[8]
    first, second = halves(sc_ref)
    for e in range(NE):
        at = expert_at(sc_ref, e)
        span = slice((e % 2) * ESLOT, (e % 2 + 1) * ESLOT)
        for h, cols in enumerate((first, second)):
            part = slice(h * HALF, (h + 1) * HALF)
            d_ref[at, :, cols] = mm_tn(hid[0][e // 2][span, :], c0_ref[e, :, part]) + mm_tn(
                hid[1][e // 2][span, :], c1_ref[e, :, part]
            )


def d_up_body(sc_ref, x0_ref, x1_ref, *refs):
    grads, d_ref = (refs[0:4], refs[4:8]), refs[8]
    first, second = halves(sc_ref)
    for e in range(NE):
        at = expert_at(sc_ref, e)
        span = slice((e % 2) * ESLOT, (e % 2 + 1) * ESLOT)
        for h, cols in enumerate((first, second)):
            part = slice(h * HALF, (h + 1) * HALF)
            d_ref[at, cols, :] = mm_tn(x0_ref[e, :, part], grads[0][e // 2][span, :]) + mm_tn(
                x1_ref[e, :, part], grads[1][e // 2][span, :]
            )


def d_sel_body(sc_ref, x0_ref, x1_ref, *refs):
    grads, code_ref, sel_ref = (refs[0:4], refs[4:8]), refs[8], refs[9]
    first, second = halves(sc_ref)
    rows = [logit_rows([g[OWN:, :] for g in grads[p]]).astype(BF) for p in range(2)]
    for e in range(NE):
        at = expert_at(sc_ref, e)
        d_sel = (mm(rows[0], x0_ref[e]) + mm(rows[1], x1_ref[e]))[e : e + 1, :]
        sel_ref[pl.ds(at, 1), first] = d_sel[:, :HALF]
        sel_ref[pl.ds(at, 1), second] = d_sel[:, HALF:]
    value = jnp.concatenate([sel_ref[:, :HALF], sel_ref[:, HALF:]], axis=0)
    high = value.astype(BF)
    code_ref[: 2 * NE, :] = high
    code_ref[2 * NE :, :] = (value - high.astype(F32)).astype(BF)


def last_sum_body(sc_ref, cot_ref, state_ref, t0, t1, t2, t3, mine_ref, rest_ref):
    core = sc_ref[1]
    terms = (t0, t1, t2, t3)
    for out_ref, side in ((mine_ref, core), (rest_ref, 1 - core)):
        for k, base_ref in enumerate((cot_ref, state_ref)):
            total = base_ref[pl.ds(pl.multiple_of(side * TOK, TOK), TOK), :].astype(F32)
            for term in terms:
                total = total + term[pl.ds(pl.multiple_of((2 * k + side) * TOK, TOK), TOK), :].astype(F32)
            out_ref[k * TOK : (k + 1) * TOK, :] = total.astype(BF)
    for d in range(4):
        rest_ref[(2 + d) * TOK : (3 + d) * TOK, :] = terms[(4 - d) % 4][4 * TOK :, :]


def last_order_body(sc_ref, mine_ref, own_ref, got_ref, cot_ref, state_ref, d_sel_ref, all_ref):
    core = sc_ref[1]
    first, second = halves(sc_ref)
    for k, out_ref in enumerate((cot_ref, state_ref)):
        out_ref[:, first] = mine_ref[k * TOK : (k + 1) * TOK, :]
        out_ref[:, second] = got_ref[k * TOK : (k + 1) * TOK, :]
    for source, side in ((own_ref, core), (got_ref, 1 - core)):
        for d1 in range(4):
            for d2 in range(4):
                x = lax.rem(sc_ref[2] + jnp.where(side == 0, d1, d2), 4)
                z = lax.rem(sc_ref[3] + jnp.where(side == 0, d2, d1), 4)
                to = pl.ds(pl.multiple_of(((x * 4 + z) * 2 + side) * NE, NE), NE)
                at = 2 * TOK + (d1 * 4 + d2) * 32
                block = source[at : at + 32, :].astype(F32)
                value = block[: 2 * NE] + block[2 * NE :]
                all_ref[to, :HALF] = value[:NE]
                all_ref[to, HALF:] = value[NE:]
    d_sel_ref[:, :] = all_ref[:, :].T


def add_swapped_body(own_ref, got_ref, *refs):
    riders, outs = refs[:-4], refs[-4:]
    for g in range(GROUPS):
        span = slice(g * GTOK, (g + 1) * GTOK)
        outs[g][:GTOK, :] = (own_ref[span, :].astype(F32) + got_ref[span, :].astype(F32)).astype(BF)
        for rider in riders:
            outs[g][GTOK:, :] = rider[:, :]


def add_second_body(count, *refs):
    outs = refs[-4:]
    for k in range(count):
        got = refs[4 * k : 4 * k + 4]
        for i in range(4):
            span = slice(i * 256, (i + 1) * 256)
            outs[i][k * 256 : (k + 1) * 256, :] = sum(r[span, :].astype(F32) for r in got).astype(BF)
    if refs[0].shape[0] > GTOK:
        for d in range(4):
            rider = refs[(4 - d) % 4][GTOK:, :]
            for out in outs:
                out[256 * count + 32 * d : 256 * count + 32 * (d + 1), :] = rider


def total_body(a, b, c, d, out_ref):
    out_ref[:, :] = sum(r[:, :].astype(F32) for r in (a, b, c, d)).astype(BF)


def advance_body(base_ref, t0, t1, t2, t3, out_ref):
    step = base_ref.shape[0] // 4
    for j in range(4):
        total = base_ref[j * step : j * step + 256, :].astype(F32)
        for d, term in enumerate((t0, t1, t2, t3)):
            at = (j - d) % 4 * 256
            total = total + term[at : at + 256, :].astype(F32)
        out_ref[j * 256 : (j + 1) * 256, :] = total.astype(BF)


def in_order(got):
    got = dict(zip(ORDER, tie(*[got[d] for d in ORDER])))
    return [got[d] for d in (1, 2, 3)]


def gather_second(stacked):
    own = {d: hop(stacked, 2, -d) for d in ORDER}
    return [stacked, own[1], own[2], own[3]]


def gather_first(mine):
    got = {d: hop(mine, 1, -d) for d in ORDER}
    return jnp.concatenate([mine, *in_order(got)], axis=0)


def scatter_first(own, oth, *riders):
    rows = GTOK + sum(r.shape[0] for r in riders)
    outs = [shape((rows, HALF), BF)] * 4
    return call(add_swapped_body, outs, (own, swap(oth), *riders), moved=6 << 20)


def scatter_second(second):
    return [second[0], *in_order({d: hop(second[d], 2, d) for d in ORDER})]


def advance(base, got):
    total = call(total_body, shape((GTOK, HALF), BF), got, moved=3 << 20)
    terms = [total, *in_order({d: hop(total, 1, -d) for d in ORDER})]
    return call(advance_body, shape((GTOK, HALF), BF), (base, *terms), moved=3 << 20)


def add_second(*sums):
    rows = 2 * TOK * len(sums) + (128 if sums[0][0].shape[0] > GTOK else 0)
    body = functools.partial(add_second_body, len(sums))
    return call(body, [shape((rows, HALF), BF)] * 4, sum(sums, []), moved=3 << 20)


def scatter_third(first):
    return [first[0], *in_order({d: hop(first[d], 1, d) for d in ORDER})]


def all_dp(block):
    return [block, *in_order({d: hop_dp(block, -d) for d in ORDER})]


def to_dp(parts):
    return [parts[0], *in_order({d: hop_dp(parts[d], d) for d in ORDER})]


def per_device(tokens, picks, halting, w_sel, w_up, w_down, cotangent):
    dp = lax.axis_index("dp")
    place = lax.axis_index("expert")
    core = lax.rem(place, 2)
    sc = jnp.stack([dp, core, place // 8, lax.rem(place // 2, 4)]).astype(jnp.int32)
    rel = lax.rem(2 * dp + jnp.arange(NE, dtype=jnp.int32), NE) + NE * place
    eid = jnp.broadcast_to(rel.astype(F32)[:, None], (NE, 256))
    sel = w_sel.T[rel]
    sel = jnp.where(core == 0, sel, jnp.concatenate([sel[:, HALF:], sel[:, :HALF]], axis=1))

    def mine_of(array):
        return jnp.where(core == 0, array[:, :HALF], array[:, HALF:])

    def rest_of(array):
        return jnp.where(core == 0, array[:, HALF:], array[:, :HALF])

    def by_core(mine, rest):
        return jnp.where(core == 0, jnp.concatenate([mine, rest], axis=0), jnp.concatenate([rest, mine], axis=0))

    live = halting[None, :, None] > jnp.arange(2, dtype=jnp.int32)[:, None, None]
    named = jnp.where(live, picks, EXPERTS).transpose(2, 0, 1).reshape(16, 256).astype(BF)
    rest = swap(jnp.concatenate([rest_of(tokens), named], axis=0))
    state = by_core(mine_of(tokens), rest[:TOK])
    stacked = gather_first(jnp.concatenate([state, by_core(named, rest[TOK:])], axis=0))
    own = gather_second(stacked)
    oth = [swap(q) for q in own]
    v = call(
        routing_body,
        shape((2, GROUPS, NE, GTOK), F32),
        (eid, *own),
        moved=1 << 20,
    )

    rows_type = shape((NE, ESLOT, 2 * HALF), BF)
    gather_flops = 2 * 640 * 1024 * 512 * 4 + 2 * 2560 * 512 * 256

    def project_up(v, own, oth):
        return call(
            up_body,
            [rows_type] + [shape((OWN + EXT, HID), BF)] * 4,
            (sc, v, sel, w_up, *own, *oth),
            flops=gather_flops,
            moved=12 << 20,
            smem=1,
        )

    def project_cot(v, own, oth):
        return call(
            down_grad_body,
            [rows_type] + [shape((OWN, HID), BF)] * 4,
            (sc, v, w_down, *own, *oth),
            flops=gather_flops,
            moved=12 << 20,
            smem=1,
        )

    def settle(parts):
        outs = [shape((OWN, HID), BF), shape((OWN, HID), F32), shape((OWN, TOK), F32)]
        return call(settle_body, outs, parts, moved=3 << 20)

    def settle_grad(parts, pre, gate):
        return call(settle_grad_body, shape((OWN + EXT, HID), BF), (*parts, pre, gate), moved=3 << 20)

    def put_of(v):
        return call(put_body, shape((QUADS, QTOK, QSLOT), BF), (v,), flops=4096 * 384 * 256, moved=4 << 20)

    y_type = shape((GROUPS * GTOK, HALF), BF)
    out_scratch = [pltpu.VMEM((QUADS, QSLOT, HALF), BF)]

    def both(body, ins, last):
        def half(far, last):
            return call(
                functools.partial(body, far),
                y_type,
                (*ins, *last),
                flops=gather_flops // 2,
                moved=8 << 20,
                scratch=out_scratch,
                smem=1,
            )

        far = half(True, last)
        far, last = tie(far, last)
        return half(False, last), far

    def outputs(put, hid):
        return both(down_body, (sc, put, w_down), hid)

    def grads_in(put, grads):
        return both(up_grad_body, (sc, sel, put, w_up), grads)

    x0, *parts = project_up(v[0], own, oth)
    parts, cotangent = tie(parts, cotangent)
    cot = by_core(mine_of(cotangent), swap(rest_of(cotangent)))
    cot_stacked = gather_first(cot)
    parts = to_dp(parts)
    parts, cot_stacked = tie(parts, cot_stacked)
    hid0, pre0, gate0 = settle(parts)
    put0, put1 = put_of(v[0]), put_of(v[1])
    hid0, cot_stacked = tie(hid0, cot_stacked)
    hid0 = all_dp(hid0)
    cot_own = gather_second(cot_stacked)
    hid0, put0, put1, cot_own = tie(hid0, put0, put1, cot_own)
    second = scatter_first(*outputs(put0, hid0))
    second, cot_own = tie(second, cot_own)
    got = scatter_second(second)
    c1, *cot_parts = project_cot(v[1], cot_own, [swap(q) for q in cot_own])
    got, cot_parts = tie(got, cot_parts)
    state1 = advance(stacked, got)

    state1, cot_parts = tie(state1, cot_parts)
    own = gather_second(state1)
    cot_parts = to_dp(cot_parts)
    own[2], cot_parts = tie(own[2], cot_parts)
    x1, *parts = project_up(v[1], own, [swap(q) for q in own])
    hid1, pre1, gate1 = settle(to_dp(parts))
    grad1 = all_dp(settle_grad(cot_parts, pre1, gate1))

    hid1, grad1 = tie(hid1, grad1)
    second = scatter_first(*grads_in(put1, grad1))
    second, hid1 = tie(second, hid1)
    got = scatter_second(second)
    hid1 = {0: hid1, 2: hop_dp(hid1, -2)}
    got, hid1 = tie(got, hid1)
    cot1, hid1[0] = tie(advance(cot_stacked, got), hid1[0])
    own = gather_second(cot1)
    hid1[1], hid1[3] = hop_dp(hid1[0], -1), hop_dp(hid1[0], -3)
    own[2], hid1 = tie(own[2], hid1)
    hid1 = [hid1[d] for d in range(4)]

    c0, *cot_parts = project_cot(v[0], own, [swap(q) for q in own])
    cot_parts, hid1 = tie(cot_parts, hid1)
    cot_parts = to_dp(cot_parts)
    out1 = outputs(put1, hid1)
    grad0 = settle_grad(cot_parts, pre0, gate0)
    grad0, second, c0 = tie(grad0, scatter_first(*out1), c0)
    grad0 = all_dp(grad0)
    state_got = scatter_second(second)
    d_down = call(
        d_down_body,
        shape(w_down.shape, F32),
        (sc, c0, c1, *hid0, *hid1),
        flops=4 * 2560 * 512 * 256,
        moved=16 << 20,
        smem=1,
    )
    grad0, d_down, state_got = tie(grad0, d_down, state_got)
    near, far = grads_in(put0, grad0)
    d_sel = call(
        d_sel_body,
        shape((4 * NE, HALF), BF),
        (sc, x0, x1, *grad0, *grad1),
        moved=8 << 20,
        scratch=[pltpu.VMEM((NE, 2 * HALF), F32)],
        smem=1,
    )
    second = scatter_first(near, far, d_sel)
    second, state_got, grad0 = tie(second, state_got, grad0)
    got = scatter_second(second)
    d_up = call(
        d_up_body,
        shape(w_up.shape, F32),
        (sc, x0, x1, *grad0, *grad1),
        flops=4 * 2560 * 512 * 256,
        moved=16 << 20,
        smem=1,
    )
    got, d_up = tie(got, d_up)
    terms = scatter_third(add_second(got, state_got))
    mine, rest = call(
        last_sum_body,
        [shape((2 * TOK, HALF), BF), shape((6 * TOK, HALF), BF)],
        (sc, cot1, state1, *terms),
        smem=1,
    )
    d_tokens, layer_out, d_sel = call(
        last_order_body,
        [shape((TOK, 2 * HALF), BF)] * 2 + [shape((2 * HALF, EXPERTS), F32)],
        (sc, mine, rest, swap(rest)),
        scratch=[pltpu.VMEM((EXPERTS, 2 * HALF), F32)],
        smem=1,
    )
    return (layer_out, d_tokens, d_up, d_down, d_sel)


def solution(mesh):
    in_specs = (
        P("expert", "dp"),
        P(None, "expert", None),
        P("expert"),
        P("dp", None),
        P("expert", "dp", None),
        P("expert", None, "dp"),
        P("expert", "dp"),
    )
    out_specs = (
        P("expert", "dp"),
        P("expert", "dp"),
        P("expert", "dp", None),
        P("expert", None, "dp"),
        P("dp", None),
    )
    return jax.shard_map(
        per_device, mesh=mesh, in_specs=in_specs, out_specs=out_specs, check_vma=False
    )
```

```python
import functools

import jax
import jax.numpy as jnp
from jax import lax
from jax.experimental import pallas as pl
from jax.experimental.pallas import tpu as pltpu
from jax.sharding import PartitionSpec as P

BF = jnp.bfloat16
F32 = jnp.float32
GELU_C = 0.7978845608028654
GELU_A = 0.044715

TOK = 128
HALF = 256
HID = 256
NE = 8
CAP = 10
GRP = 8
GROUPS = 4
GTOK = GRP * TOK
GSLOT = GRP * CAP
ESLOT = GROUPS * GSLOT
OWN = 2 * ESLOT
EXT = 16
QUADS = 8
QTOK = 4 * TOK
QCAP = 4 * CAP
QSLOT = NE * QCAP
EXPERTS = 256
PIECE = 2 * TOK + 32
ORDER = (2, 1, 3)
VMEM = pl.BlockSpec(memory_space=pltpu.VMEM)
HBM = pl.BlockSpec(memory_space=pl.ANY)
SMEM = pl.BlockSpec(memory_space=pltpu.SMEM)


def dev(x, z, c):
    return (x * 4 + z) * 2 + c


PLACES = [(x, z, c) for x in range(4) for z in range(4) for c in range(2)]
SWAP = [(dev(x, z, c), dev(x, z, 1 - c)) for x, z, c in PLACES]


def along(axis, step):
    pairs = []
    for x, z, c in PLACES:
        if (axis + c) % 2 == 1:
            pairs.append((dev(x, z, c), dev((x + step) % 4, z, c)))
        else:
            pairs.append((dev(x, z, c), dev(x, (z + step) % 4, c)))
    return pairs


def hop(value, axis, step):
    return lax.ppermute(value, "expert", along(axis, step % 4))


def swap(value):
    return lax.ppermute(value, "expert", SWAP)


def hop_dp(value, step):
    return lax.ppermute(value, "dp", [(y, (y + step) % 4) for y in range(4)])


def call(body, outs, ins, flops=0, moved=1 << 20, scratch=(), smem=0, anywhere=0, outs_anywhere=(), limit=20):
    flat = [outs] if not isinstance(outs, list) else outs
    specs = [HBM if i in outs_anywhere else VMEM for i in range(len(flat))]
    return pl.pallas_call(
        body,
        out_shape=outs,
        in_specs=[SMEM] * smem + [VMEM] * (len(ins) - smem - anywhere) + [HBM] * anywhere,
        out_specs=specs if isinstance(outs, list) else specs[0],
        scratch_shapes=list(scratch),
        compiler_params=pltpu.CompilerParams(vmem_limit_bytes=limit * 1024 * 1024),
        cost_estimate=pl.CostEstimate(flops=flops, bytes_accessed=moved, transcendentals=0),
    )(*ins)


def shape(dims, dtype):
    return jax.ShapeDtypeStruct(dims, dtype)


def tie(*values):
    return lax.optimization_barrier(values)


def mm(a, b):
    return lax.dot_general(a, b, (((1,), (0,)), ((), ())), preferred_element_type=F32)


def mm_nt(a, b):
    return lax.dot_general(a, b, (((1,), (1,)), ((), ())), preferred_element_type=F32)


def mm_tn(a, b):
    return lax.dot_general(a, b, (((0,), (0,)), ((), ())), preferred_element_type=F32)


def routing_body(eid_ref, own0, own1, own2, own3, v_ref):
    own = (own0, own1, own2, own3)
    eid = eid_ref[:, :]
    marks = []
    for g in range(GROUPS):
        for j in range(GRP):
            at = j // 2 * PIECE + 2 * TOK + j % 2 * 16
            named = own[g][at : at + 16, :].astype(F32)
            mark = jnp.zeros((NE, 256), F32)
            for k in range(16):
                mark = jnp.where(named[k : k + 1, :] == eid, 1.0, mark)
            marks.append(mark)
    before = lax.broadcasted_iota(jnp.int32, (TOK, TOK), 0) < lax.broadcasted_iota(jnp.int32, (TOK, TOK), 1)
    before = jnp.where(before, 1.0, 0.0).astype(BF)
    for p in range(2):
        stacked = jnp.concatenate([m[:, p * TOK : (p + 1) * TOK] for m in marks], axis=0)
        rank = mm(stacked.astype(BF), before)
        for g in range(GROUPS):
            for j in range(GRP):
                at = (g * GRP + j) * NE
                v_ref[p, g, :, j * TOK : (j + 1) * TOK] = jnp.where(
                    stacked[at : at + NE] > 0, rank[at : at + NE] + float(CAP * (j % 4)), -1.0
                )


def put_body(v_ref, put_ref):
    at_lane = lax.broadcasted_iota(jnp.int32, (TOK, QSLOT), 1)
    at_row = lax.broadcasted_iota(jnp.int32, (TOK, QSLOT), 0)
    spread = jnp.where((at_lane >= at_row * QCAP) & (at_lane < (at_row + 1) * QCAP), 1.0, 0.0).astype(BF)
    slot = lax.rem(lax.broadcasted_iota(jnp.int32, (1, QSLOT), 1), QCAP).astype(F32)
    for q in range(QUADS):
        v = v_ref[q // 2, :, (q % 2) * QTOK : (q % 2 + 1) * QTOK]
        turned = jnp.concatenate([v, jnp.zeros((TOK - NE, QTOK), F32)], axis=0).T.astype(BF)
        put_ref[q] = jnp.where(mm(turned, spread) == slot, 1.0, 0.0).astype(BF)


def gather_rows(v_ref, near_of, far_of, x_ref):
    slot = lax.broadcasted_iota(jnp.int32, (QCAP, QTOK), 0).astype(F32)
    for g in range(GROUPS):
        rows = []
        for i in range(2):
            v = v_ref[g, :, i * QTOK : (i + 1) * QTOK]
            pick = jnp.concatenate([jnp.where(slot == v[e : e + 1, :], 1.0, 0.0) for e in range(NE)], axis=0).astype(BF)
            rows.append(
                [
                    mm(pick[:, :256], source(g, 2 * i)) + mm(pick[:, 256:], source(g, 2 * i + 1))
                    for source in (near_of, far_of)
                ]
            )
        for e in range(NE):
            at = slice(e * QCAP, (e + 1) * QCAP)
            for h in range(2):
                x_ref[e, g * GSLOT : (g + 1) * GSLOT, h * HALF : (h + 1) * HALF] = jnp.concatenate(
                    [rows[0][h][at], rows[1][h][at]], axis=0
                ).astype(BF)


def gather_pieces(v_ref, own, oth, x_ref):
    step = own[0].shape[0] // 4
    gather_rows(
        v_ref,
        lambda g, d: own[g][d * step : d * step + 256, :],
        lambda g, d: oth[d][g * step : g * step + 256, :] if len(oth) == 4 else oth[0][pl.ds((4 * d + g) * 256, 256), :],
        x_ref,
    )


def halves(sc_ref):
    core = sc_ref[1]
    return (
        pl.ds(pl.multiple_of(core * HALF, HALF), HALF),
        pl.ds(pl.multiple_of((1 - core) * HALF, HALF), HALF),
    )


def expert_at(sc_ref, e):
    return lax.rem(2 * sc_ref[0] + e, NE)


def up_body(sc_ref, v_ref, sel_ref, w_up_ref, *refs):
    own, oth, x_ref, parts = refs[0:4], refs[4:8], refs[8], refs[9:13]
    gather_pieces(v_ref, own, oth, x_ref)
    first, second = halves(sc_ref)
    sel = sel_ref[:, :]
    lane_pad = jnp.zeros((1, 192), F32)
    for dy in range(4):
        heads, tails = [], []
        for i in range(2):
            e = 2 * dy + i
            at = expert_at(sc_ref, e)
            rows = x_ref[e]
            total = mm(rows[:, :HALF], w_up_ref[at, first, :]) + mm(rows[:, HALF:], w_up_ref[at, second, :])
            parts[dy][i * ESLOT : (i + 1) * ESLOT, :] = total.astype(BF)
            logit = mm_nt(sel, rows)[e : e + 1, :]
            heads.append(logit[:, :256])
            tails.append(jnp.concatenate([logit[:, 256:], lane_pad], axis=1))
        logits = jnp.concatenate(heads + tails, axis=0)
        high = logits.astype(BF).astype(F32)
        low = logits - high
        parts[dy][OWN:, :] = jnp.concatenate([high, low, jnp.zeros((8, 256), F32)], axis=0).astype(BF)


def down_grad_body(sc_ref, v_ref, w_down_ref, *refs):
    own, oth, x_ref, parts = refs[0:4], refs[4:-5], refs[-5], refs[-4:]
    gather_pieces(v_ref, own, oth, x_ref)
    first, second = halves(sc_ref)
    for e in range(NE):
        at = expert_at(sc_ref, e)
        rows = x_ref[e]
        total = mm_nt(rows[:, :HALF], w_down_ref[at, :, first]) + mm_nt(rows[:, HALF:], w_down_ref[at, :, second])
        parts[e // 2][(e % 2) * ESLOT : (e % 2 + 1) * ESLOT, :] = total.astype(BF)


def as_columns(rows):
    turned = jnp.concatenate([rows, jnp.zeros((TOK - rows.shape[0], 256), F32)], axis=0).T
    return jnp.concatenate([turned[:, 0:1], turned[:64, 2:3], turned[:, 1:2], turned[:64, 3:4]], axis=0)


def as_rows(column):
    wide = jnp.broadcast_to(column, (OWN, TOK))
    lane = lax.broadcasted_iota(jnp.int32, (256, TOK), 1)
    pad = jnp.zeros((192, TOK), F32)
    pieces = (
        wide[0:256],
        wide[ESLOT : ESLOT + 256],
        jnp.concatenate([wide[256:ESLOT], pad], axis=0),
        jnp.concatenate([wide[ESLOT + 256 :], pad], axis=0),
    )
    mixed = jnp.zeros((256, TOK), F32)
    for i, piece in enumerate(pieces):
        mixed = jnp.where(lane == i, piece, mixed)
    return mixed.T[:EXT]


def settle_body(p0, p1, p2, p3, hid_ref, pre_ref, gate_ref):
    def total(lo, hi):
        return sum(p[lo:hi, :].astype(F32) for p in (p0, p1, p2, p3))

    extra = total(OWN, OWN + EXT)
    gate = jax.nn.sigmoid(as_columns(extra[0:4] + extra[4:8]))
    pre = total(0, OWN)
    pre_ref[:, :] = pre
    gate_ref[:, :] = jnp.broadcast_to(gate, (OWN, TOK))
    inner = GELU_C * (pre + GELU_A * pre * pre * pre)
    hid_ref[:, :] = (gate * (0.5 * pre * (1.0 + jnp.tanh(inner)))).astype(BF)


def settle_grad_body(*refs):
    parts, (pre_ref, gate_ref, grad_ref) = refs[:-3], refs[-3:]
    total = sum(p[:, :].astype(F32) for p in parts)
    pre = pre_ref[:, :]
    gate = gate_ref[:, 0:1]
    tangent = jnp.tanh(GELU_C * (pre + GELU_A * pre * pre * pre))
    hidden = (0.5 * pre * (1.0 + tangent)).astype(BF).astype(F32)
    slope = 0.5 * (1.0 + tangent) + 0.5 * pre * (1.0 - tangent * tangent) * GELU_C * (1.0 + 3.0 * GELU_A * pre * pre)
    score = jnp.sum(hidden * total, axis=1, keepdims=True)
    grad_ref[0:OWN, :] = (gate * total * slope).astype(BF)
    grad_ref[OWN:, :] = as_rows(score * gate * (1.0 - gate)).astype(BF)


def place_rows(out_ref, e, pair):
    for q in range(QUADS):
        span = slice(q * QCAP, (q + 1) * QCAP)
        out_ref[q, e * QCAP : (e + 2) * QCAP, :] = jnp.concatenate([pair[0][span], pair[1][span]], axis=0).astype(BF)


def scatter_rows(far, put_ref, out_ref, y_ref):
    for q in range(QUADS):
        rows = mm(put_ref[q], out_ref[q]).astype(BF)
        g, i = q // 2, q % 2
        for k in range(2):
            at = ((2 * i + k) * 4 + g if far else 2 * q + k) * 256
            y_ref[at : at + 256, :] = rows[k * 256 : (k + 1) * 256]


def down_body(far, sc_ref, put_ref, w_down_ref, h0, h1, h2, h3, y_ref, out_ref):
    hid = (h0, h1, h2, h3)
    cols = halves(sc_ref)[int(far)]
    for d in range(4):
        pair = [
            mm(hid[d][i * ESLOT : (i + 1) * ESLOT, :], w_down_ref[expert_at(sc_ref, 2 * d + i), :, cols])
            for i in range(2)
        ]
        place_rows(out_ref, 2 * d, pair)
    scatter_rows(far, put_ref, out_ref, y_ref)


def logit_rows(extras):
    rows = []
    for extra in extras:
        extra = extra.astype(F32)
        for i in range(2):
            rows.append(jnp.concatenate([extra[i : i + 1, :], extra[2 + i : 3 + i, :64]], axis=1))
    return jnp.concatenate(rows, axis=0)


def up_grad_body(far, sc_ref, sel_ref, put_ref, w_up_ref, h0, h1, h2, h3, y_ref, out_ref):
    grads = (h0, h1, h2, h3)
    part = slice(HALF, 2 * HALF) if far else slice(0, HALF)
    cols = halves(sc_ref)[int(far)]
    sel = sel_ref[:, part].astype(F32)
    rows = logit_rows([g[OWN:, :] for g in grads])
    rows = jnp.concatenate([rows, jnp.zeros((NE, 64), F32)], axis=1)
    columns = jnp.concatenate([rows, jnp.zeros((TOK - NE, 384), F32)], axis=0).T
    for d in range(4):
        pair = []
        for i in range(2):
            e = 2 * d + i
            out = mm_nt(grads[d][i * ESLOT : (i + 1) * ESLOT, :], w_up_ref[expert_at(sc_ref, e), cols, :])
            pair.append(out + columns[:ESLOT, e : e + 1] * sel[e : e + 1, :])
        place_rows(out_ref, 2 * d, pair)
    scatter_rows(far, put_ref, out_ref, y_ref)


def d_down_body(sc_ref, c0_ref, c1_ref, *refs):
    hid, d_ref = (refs[0:4], refs[4:8]), refs[8]
    first, second = halves(sc_ref)
    for e in range(NE):
        at = expert_at(sc_ref, e)
        span = slice((e % 2) * ESLOT, (e % 2 + 1) * ESLOT)
        for h, cols in enumerate((first, second)):
            part = slice(h * HALF, (h + 1) * HALF)
            d_ref[at, :, cols] = mm_tn(hid[0][e // 2][span, :], c0_ref[e, :, part]) + mm_tn(
                hid[1][e // 2][span, :], c1_ref[e, :, part]
            )


def d_up_body(sc_ref, x0_ref, x1_ref, *refs):
    grads, d_ref = (refs[0:4], refs[4:8]), refs[8]
    first, second = halves(sc_ref)
    for e in range(NE):
        at = expert_at(sc_ref, e)
        span = slice((e % 2) * ESLOT, (e % 2 + 1) * ESLOT)
        for h, cols in enumerate((first, second)):
            part = slice(h * HALF, (h + 1) * HALF)
            d_ref[at, cols, :] = mm_tn(x0_ref[e, :, part], grads[0][e // 2][span, :]) + mm_tn(
                x1_ref[e, :, part], grads[1][e // 2][span, :]
            )


def d_sel_body(sc_ref, x0_ref, x1_ref, *refs):
    grads, code_ref, sel_ref = (refs[0:4], refs[4:8]), refs[8], refs[9]
    first, second = halves(sc_ref)
    rows = [logit_rows([g[OWN:, :] for g in grads[p]]).astype(BF) for p in range(2)]
    for e in range(NE):
        at = expert_at(sc_ref, e)
        d_sel = (mm(rows[0], x0_ref[e]) + mm(rows[1], x1_ref[e]))[e : e + 1, :]
        sel_ref[pl.ds(at, 1), first] = d_sel[:, :HALF]
        sel_ref[pl.ds(at, 1), second] = d_sel[:, HALF:]
    value = jnp.concatenate([sel_ref[:, :HALF], sel_ref[:, HALF:]], axis=0)
    high = value.astype(BF)
    code_ref[: 2 * NE, :] = high
    code_ref[2 * NE :, :] = (value - high.astype(F32)).astype(BF)


def last_sum_body(sc_ref, cot_ref, state_ref, t0, t1, t2, t3, mine_ref, rest_ref):
    core = sc_ref[1]
    terms = (t0, t1, t2, t3)
    for out_ref, side in ((mine_ref, core), (rest_ref, 1 - core)):
        for k, base_ref in enumerate((cot_ref, state_ref)):
            total = base_ref[pl.ds(pl.multiple_of(side * TOK, TOK), TOK), :].astype(F32)
            for term in terms:
                total = total + term[pl.ds(pl.multiple_of((2 * k + side) * TOK, TOK), TOK), :].astype(F32)
            out_ref[k * TOK : (k + 1) * TOK, :] = total.astype(BF)
    for d in range(4):
        rest_ref[(2 + d) * TOK : (3 + d) * TOK, :] = terms[(4 - d) % 4][4 * TOK :, :]


def last_order_body(sc_ref, mine_ref, own_ref, got_ref, cot_ref, state_ref, d_sel_ref, all_ref):
    core = sc_ref[1]
    first, second = halves(sc_ref)
    for k, out_ref in enumerate((cot_ref, state_ref)):
        out_ref[:, first] = mine_ref[k * TOK : (k + 1) * TOK, :]
        out_ref[:, second] = got_ref[k * TOK : (k + 1) * TOK, :]
    for source, side in ((own_ref, core), (got_ref, 1 - core)):
        for d1 in range(4):
            for d2 in range(4):
                x = lax.rem(sc_ref[2] + jnp.where(side == 0, d1, d2), 4)
                z = lax.rem(sc_ref[3] + jnp.where(side == 0, d2, d1), 4)
                to = pl.ds(pl.multiple_of(((x * 4 + z) * 2 + side) * NE, NE), NE)
                at = 2 * TOK + (d1 * 4 + d2) * 32
                block = source[at : at + 32, :].astype(F32)
                value = block[: 2 * NE] + block[2 * NE :]
                all_ref[to, :HALF] = value[:NE]
                all_ref[to, HALF:] = value[NE:]
    d_sel_ref[:, :] = all_ref[:, :].T


def add_swapped_body(own_ref, got_ref, *refs):
    riders, outs = refs[:-4], refs[-4:]
    for g in range(GROUPS):
        span = slice(g * GTOK, (g + 1) * GTOK)
        outs[g][:GTOK, :] = (own_ref[span, :].astype(F32) + got_ref[span, :].astype(F32)).astype(BF)
        for rider in riders:
            outs[g][GTOK:, :] = rider[:, :]


def add_second_body(count, *refs):
    outs = refs[-4:]
    for k in range(count):
        got = refs[4 * k : 4 * k + 4]
        for i in range(4):
            span = slice(i * 256, (i + 1) * 256)
            outs[i][k * 256 : (k + 1) * 256, :] = sum(r[span, :].astype(F32) for r in got).astype(BF)
    if refs[0].shape[0] > GTOK:
        for d in range(4):
            rider = refs[(4 - d) % 4][GTOK:, :]
            for out in outs:
                out[256 * count + 32 * d : 256 * count + 32 * (d + 1), :] = rider


def total_body(a, b, c, d, out_ref):
    out_ref[:, :] = sum(r[:, :].astype(F32) for r in (a, b, c, d)).astype(BF)


def advance_body(base_ref, t0, t1, t2, t3, out_ref):
    step = base_ref.shape[0] // 4
    for j in range(4):
        total = base_ref[j * step : j * step + 256, :].astype(F32)
        for d, term in enumerate((t0, t1, t2, t3)):
            at = (j - d) % 4 * 256
            total = total + term[at : at + 256, :].astype(F32)
        out_ref[j * 256 : (j + 1) * 256, :] = total.astype(BF)


def in_order(got):
    got = dict(zip(ORDER, tie(*[got[d] for d in ORDER])))
    return [got[d] for d in (1, 2, 3)]


def gather_second(stacked):
    own = {d: hop(stacked, 2, -d) for d in ORDER}
    return [stacked, own[1], own[2], own[3]]


def gather_first(mine):
    got = {d: hop(mine, 1, -d) for d in ORDER}
    return jnp.concatenate([mine, *in_order(got)], axis=0)


def scatter_first(own, oth, *riders):
    rows = GTOK + sum(r.shape[0] for r in riders)
    outs = [shape((rows, HALF), BF)] * 4
    return call(add_swapped_body, outs, (own, swap(oth), *riders), moved=6 << 20)


def scatter_second(second):
    return [second[0], *in_order({d: hop(second[d], 2, d) for d in ORDER})]


def stack_body(a, b, c, d, out_ref):
    for i, piece in enumerate((a, b, c, d)):
        out_ref[i * PIECE : (i + 1) * PIECE, :] = piece[:, :]


def no_work(values):
    return values


def advance(base, got, beside=no_work, values=()):
    total = call(total_body, shape((GTOK, HALF), BF), got, moved=3 << 20)
    total, values = tie(total, values)
    terms = [total, *in_order({d: hop(total, 1, -d) for d in ORDER})]
    terms, values = tie(terms, beside(values))
    return call(advance_body, shape((GTOK, HALF), BF), (base, *terms), moved=3 << 20), values


def add_second(*sums):
    rows = 2 * TOK * len(sums) + (128 if sums[0][0].shape[0] > GTOK else 0)
    body = functools.partial(add_second_body, len(sums))
    return call(body, [shape((rows, HALF), BF)] * 4, sum(sums, []), moved=3 << 20)


def scatter_third(first):
    return [first[0], *in_order({d: hop(first[d], 1, d) for d in ORDER})]


def all_dp(block):
    return [block, *in_order({d: hop_dp(block, -d) for d in ORDER})]


def to_dp(parts):
    return [parts[0], *in_order({d: hop_dp(parts[d], d) for d in ORDER})]


def per_device(tokens, picks, halting, w_sel, w_up, w_down, cotangent):
    dp = lax.axis_index("dp")
    place = lax.axis_index("expert")
    core = lax.rem(place, 2)
    sc = jnp.stack([dp, core, place // 8, lax.rem(place // 2, 4)]).astype(jnp.int32)
    rel = lax.rem(2 * dp + jnp.arange(NE, dtype=jnp.int32), NE) + NE * place
    eid = jnp.broadcast_to(rel.astype(F32)[:, None], (NE, 256))
    sel = w_sel.T[rel]
    sel = jnp.where(core == 0, sel, jnp.concatenate([sel[:, HALF:], sel[:, :HALF]], axis=1))

    def mine_of(array):
        return jnp.where(core == 0, array[:, :HALF], array[:, HALF:])

    def rest_of(array):
        return jnp.where(core == 0, array[:, HALF:], array[:, :HALF])

    def by_core(mine, rest):
        return jnp.where(core == 0, jnp.concatenate([mine, rest], axis=0), jnp.concatenate([rest, mine], axis=0))

    live = halting[None, :, None] > jnp.arange(2, dtype=jnp.int32)[:, None, None]
    named = jnp.where(live, picks, EXPERTS).transpose(2, 0, 1).reshape(16, 256).astype(BF)
    rest = swap(jnp.concatenate([rest_of(tokens), named], axis=0))
    state = by_core(mine_of(tokens), rest[:TOK])
    stacked = jnp.concatenate([state, by_core(named, rest[TOK:])], axis=0)
    stacked = [stacked, *in_order({d: hop(stacked, 1, -d) for d in ORDER})]
    stacked = call(stack_body, shape((4 * PIECE, HALF), BF), stacked)
    stacked, cotangent = tie(stacked, cotangent)
    own = gather_second(stacked)
    cot = by_core(mine_of(cotangent), swap(rest_of(cotangent)))
    cot_stacked = gather_first(cot)
    own[2], cot_stacked = tie(own[2], cot_stacked)
    oth = [swap(q) for q in own]
    v = call(
        routing_body,
        shape((2, GROUPS, NE, GTOK), F32),
        (eid, *own),
        moved=1 << 20,
    )

    rows_type = shape((NE, ESLOT, 2 * HALF), BF)
    gather_flops = 2 * 640 * 1024 * 512 * 4 + 2 * 2560 * 512 * 256

    def project_up(v, own, oth):
        return call(
            up_body,
            [rows_type] + [shape((OWN + EXT, HID), BF)] * 4,
            (sc, v, sel, w_up, *own, *oth),
            flops=gather_flops,
            moved=12 << 20,
            smem=1,
        )

    def project_cot(v, own, oth):
        return call(
            down_grad_body,
            [rows_type] + [shape((OWN, HID), BF)] * 4,
            (sc, v, w_down, *own, *oth),
            flops=gather_flops,
            moved=12 << 20,
            smem=1,
        )

    def settle(parts):
        outs = [shape((OWN, HID), BF), shape((OWN, HID), F32), shape((OWN, TOK), F32)]
        return call(settle_body, outs, parts, moved=3 << 20)

    def settle_grad(parts, pre, gate):
        return call(settle_grad_body, shape((OWN + EXT, HID), BF), (*parts, pre, gate), moved=3 << 20)

    def put_of(v):
        return call(put_body, shape((QUADS, QTOK, QSLOT), BF), (v,), flops=4096 * 384 * 256, moved=4 << 20)

    y_type = shape((GROUPS * GTOK, HALF), BF)
    out_scratch = [pltpu.VMEM((QUADS, QSLOT, HALF), BF)]

    def both(body, ins, last):
        def half(far, last):
            return call(
                functools.partial(body, far),
                y_type,
                (*ins, *last),
                flops=gather_flops // 2,
                moved=8 << 20,
                scratch=out_scratch,
                smem=1,
            )

        far = half(True, last)
        far, last = tie(far, last)
        return half(False, last), far

    def outputs(put, hid):
        return both(down_body, (sc, put, w_down), hid)

    def grads_in(put, grads):
        return both(up_grad_body, (sc, sel, put, w_up), grads)

    x0, *parts = project_up(v[0], own, oth)
    parts, cot_stacked = tie(parts, cot_stacked)
    parts = to_dp(parts)
    cot_own = gather_second(cot_stacked)
    parts, cot_own = tie(parts, cot_own)
    hid0, pre0, gate0 = settle(parts)
    put0, put1 = put_of(v[0]), put_of(v[1])
    hid0, cot_own = tie(hid0, cot_own)
    hid0 = all_dp(hid0)
    cot_far = swap(jnp.concatenate(cot_own, axis=0))
    hid0, put0, put1, cot_own, cot_far = tie(hid0, put0, put1, cot_own, cot_far)
    near, far = outputs(put0, hid0)
    near, cot_own, cot_far = tie(near, cot_own, cot_far)
    c1, *cot_parts = project_cot(v[1], cot_own, [cot_far])
    near, cot_parts = tie(near, cot_parts)
    second, cot_parts = tie(scatter_first(near, far), cot_parts)
    got = scatter_second(second)
    cot_parts[2] = hop_dp(cot_parts[2], 2)
    got, cot_parts[2] = tie(got, cot_parts[2])
    state1, (cot_parts[1], cot_parts[3]) = advance(
        stacked, got, lambda two: (hop_dp(two[0], 1), hop_dp(two[1], 3)), (cot_parts[1], cot_parts[3])
    )

    own = gather_second(state1)
    x1, *parts = project_up(v[1], own, [swap(q) for q in own])
    hid1, pre1, gate1 = settle(to_dp(parts))
    grad1 = all_dp(settle_grad(cot_parts, pre1, gate1))

    hid1, grad1 = tie(hid1, grad1)
    second = scatter_first(*grads_in(put1, grad1))
    second, hid1 = tie(second, hid1)
    got = scatter_second(second)
    hid1 = {0: hid1, 2: hop_dp(hid1, -2)}
    got, hid1 = tie(got, hid1)
    cot1, hid1 = advance(
        cot_stacked, got, lambda hid: {**hid, 1: hop_dp(hid[0], -1), 3: hop_dp(hid[0], -3)}, hid1
    )
    hid1 = [hid1[d] for d in range(4)]
    own = gather_second(cot1)

    c0, *cot_parts = project_cot(v[0], own, [swap(q) for q in own])
    cot_parts, hid1 = tie(cot_parts, hid1)
    cot_parts = to_dp(cot_parts)
    out1 = outputs(put1, hid1)
    grad0 = settle_grad(cot_parts, pre0, gate0)
    grad0, second, c0 = tie(grad0, scatter_first(*out1), c0)
    grad0 = all_dp(grad0)
    state_got = scatter_second(second)
    d_down = call(
        d_down_body,
        shape(w_down.shape, F32),
        (sc, c0, c1, *hid0, *hid1),
        flops=4 * 2560 * 512 * 256,
        moved=16 << 20,
        smem=1,
    )
    grad0, d_down, state_got = tie(grad0, d_down, state_got)
    near, far = grads_in(put0, grad0)
    d_sel = call(
        d_sel_body,
        shape((4 * NE, HALF), BF),
        (sc, x0, x1, *grad0, *grad1),
        moved=8 << 20,
        scratch=[pltpu.VMEM((NE, 2 * HALF), F32)],
        smem=1,
    )
    second = scatter_first(near, far, d_sel)
    second, state_got, grad0 = tie(second, state_got, grad0)
    got = scatter_second(second)
    d_up = call(
        d_up_body,
        shape(w_up.shape, F32),
        (sc, x0, x1, *grad0, *grad1),
        flops=4 * 2560 * 512 * 256,
        moved=16 << 20,
        smem=1,
    )
    got, d_up = tie(got, d_up)
    terms = scatter_third(add_second(got, state_got))
    mine, rest = call(
        last_sum_body,
        [shape((2 * TOK, HALF), BF), shape((6 * TOK, HALF), BF)],
        (sc, cot1, state1, *terms),
        smem=1,
    )
    d_tokens, layer_out, d_sel = call(
        last_order_body,
        [shape((TOK, 2 * HALF), BF)] * 2 + [shape((2 * HALF, EXPERTS), F32)],
        (sc, mine, rest, swap(rest)),
        scratch=[pltpu.VMEM((EXPERTS, 2 * HALF), F32)],
        smem=1,
    )
    return (layer_out, d_tokens, d_up, d_down, d_sel)


def solution(mesh):
    in_specs = (
        P("expert", "dp"),
        P(None, "expert", None),
        P("expert"),
        P("dp", None),
        P("expert", "dp", None),
        P("expert", None, "dp"),
        P("expert", "dp"),
    )
    out_specs = (
        P("expert", "dp"),
        P("expert", "dp"),
        P("expert", "dp", None),
        P("expert", None, "dp"),
        P("dp", None),
    )
    return jax.shard_map(
        per_device, mesh=mesh, in_specs=in_specs, out_specs=out_specs, check_vma=False
    )
```

```python
import functools

import jax
import jax.numpy as jnp
from jax import lax
from jax.experimental import pallas as pl
from jax.experimental.pallas import tpu as pltpu
from jax.sharding import PartitionSpec as P

BF = jnp.bfloat16
F32 = jnp.float32
GELU_C = 0.7978845608028654
GELU_A = 0.044715

TOK = 128
HALF = 256
HID = 256
NE = 8
CAP = 10
GRP = 8
GROUPS = 4
GTOK = GRP * TOK
GSLOT = GRP * CAP
ESLOT = GROUPS * GSLOT
OWN = 2 * ESLOT
EXT = 16
QUADS = 8
QTOK = 4 * TOK
QCAP = 4 * CAP
QSLOT = NE * QCAP
EXPERTS = 256
PIECE = 2 * TOK + 32
ORDER = (2, 1, 3)
VMEM = pl.BlockSpec(memory_space=pltpu.VMEM)
HBM = pl.BlockSpec(memory_space=pl.ANY)
SMEM = pl.BlockSpec(memory_space=pltpu.SMEM)


def dev(x, z, c):
    return (x * 4 + z) * 2 + c


PLACES = [(x, z, c) for x in range(4) for z in range(4) for c in range(2)]
SWAP = [(dev(x, z, c), dev(x, z, 1 - c)) for x, z, c in PLACES]


def along(axis, step):
    pairs = []
    for x, z, c in PLACES:
        if (axis + c) % 2 == 1:
            pairs.append((dev(x, z, c), dev((x + step) % 4, z, c)))
        else:
            pairs.append((dev(x, z, c), dev(x, (z + step) % 4, c)))
    return pairs


def hop(value, axis, step):
    return lax.ppermute(value, "expert", along(axis, step % 4))


def swap(value):
    return lax.ppermute(value, "expert", SWAP)


def hop_dp(value, step):
    return lax.ppermute(value, "dp", [(y, (y + step) % 4) for y in range(4)])


def call(body, outs, ins, flops=0, moved=1 << 20, scratch=(), smem=0, anywhere=0, outs_anywhere=(), limit=20):
    flat = [outs] if not isinstance(outs, list) else outs
    specs = [HBM if i in outs_anywhere else VMEM for i in range(len(flat))]
    return pl.pallas_call(
        body,
        out_shape=outs,
        in_specs=[SMEM] * smem + [VMEM] * (len(ins) - smem - anywhere) + [HBM] * anywhere,
        out_specs=specs if isinstance(outs, list) else specs[0],
        scratch_shapes=list(scratch),
        compiler_params=pltpu.CompilerParams(vmem_limit_bytes=limit * 1024 * 1024),
        cost_estimate=pl.CostEstimate(flops=flops, bytes_accessed=moved, transcendentals=0),
    )(*ins)


def shape(dims, dtype):
    return jax.ShapeDtypeStruct(dims, dtype)


def tie(*values):
    return lax.optimization_barrier(values)


def mm(a, b):
    return lax.dot_general(a, b, (((1,), (0,)), ((), ())), preferred_element_type=F32)


def mm_nt(a, b):
    return lax.dot_general(a, b, (((1,), (1,)), ((), ())), preferred_element_type=F32)


def mm_tn(a, b):
    return lax.dot_general(a, b, (((0,), (0,)), ((), ())), preferred_element_type=F32)


def routing_body(eid_ref, own0, own1, own2, own3, v_ref):
    own = (own0, own1, own2, own3)
    eid = eid_ref[:, :]
    marks = []
    for g in range(GROUPS):
        for j in range(GRP):
            at = j // 2 * PIECE + 2 * TOK + j % 2 * 16
            named = own[g][at : at + 16, :].astype(F32)
            mark = jnp.zeros((NE, 256), F32)
            for k in range(16):
                mark = jnp.where(named[k : k + 1, :] == eid, 1.0, mark)
            marks.append(mark)
    before = lax.broadcasted_iota(jnp.int32, (TOK, TOK), 0) < lax.broadcasted_iota(jnp.int32, (TOK, TOK), 1)
    before = jnp.where(before, 1.0, 0.0).astype(BF)
    for p in range(2):
        stacked = jnp.concatenate([m[:, p * TOK : (p + 1) * TOK] for m in marks], axis=0)
        rank = mm(stacked.astype(BF), before)
        for g in range(GROUPS):
            for j in range(GRP):
                at = (g * GRP + j) * NE
                v_ref[p, g, :, j * TOK : (j + 1) * TOK] = jnp.where(
                    stacked[at : at + NE] > 0, rank[at : at + NE] + float(CAP * (j % 4)), -1.0
                )


def put_body(v_ref, put_ref):
    at_lane = lax.broadcasted_iota(jnp.int32, (TOK, QSLOT), 1)
    at_row = lax.broadcasted_iota(jnp.int32, (TOK, QSLOT), 0)
    spread = jnp.where((at_lane >= at_row * QCAP) & (at_lane < (at_row + 1) * QCAP), 1.0, 0.0).astype(BF)
    slot = lax.rem(lax.broadcasted_iota(jnp.int32, (1, QSLOT), 1), QCAP).astype(F32)
    for q in range(QUADS):
        v = v_ref[q // 2, :, (q % 2) * QTOK : (q % 2 + 1) * QTOK]
        turned = jnp.concatenate([v, jnp.zeros((TOK - NE, QTOK), F32)], axis=0).T.astype(BF)
        put_ref[q] = jnp.where(mm(turned, spread) == slot, 1.0, 0.0).astype(BF)


def gather_rows(v_ref, near_of, far_of, x_ref):
    slot = lax.broadcasted_iota(jnp.int32, (QCAP, QTOK), 0).astype(F32)
    for g in range(GROUPS):
        rows = []
        for i in range(2):
            v = v_ref[g, :, i * QTOK : (i + 1) * QTOK]
            pick = jnp.concatenate([jnp.where(slot == v[e : e + 1, :], 1.0, 0.0) for e in range(NE)], axis=0).astype(BF)
            rows.append(
                [
                    mm(pick[:, :256], source(g, 2 * i)) + mm(pick[:, 256:], source(g, 2 * i + 1))
                    for source in (near_of, far_of)
                ]
            )
        for e in range(NE):
            at = slice(e * QCAP, (e + 1) * QCAP)
            for h in range(2):
                x_ref[e, g * GSLOT : (g + 1) * GSLOT, h * HALF : (h + 1) * HALF] = jnp.concatenate(
                    [rows[0][h][at], rows[1][h][at]], axis=0
                ).astype(BF)


def gather_pieces(v_ref, own, oth, x_ref):
    step = own[0].shape[0] // 4
    gather_rows(
        v_ref,
        lambda g, d: own[g][d * step : d * step + 256, :],
        lambda g, d: oth[d][g * step : g * step + 256, :] if len(oth) == 4 else oth[0][pl.ds((4 * d + g) * 256, 256), :],
        x_ref,
    )


def halves(sc_ref):
    core = sc_ref[1]
    return (
        pl.ds(pl.multiple_of(core * HALF, HALF), HALF),
        pl.ds(pl.multiple_of((1 - core) * HALF, HALF), HALF),
    )


def expert_at(sc_ref, e):
    return lax.rem(2 * sc_ref[0] + e, NE)


def up_body(sc_ref, v_ref, sel_ref, w_up_ref, *refs):
    own, oth, x_ref, parts = refs[0:4], refs[4:8], refs[8], refs[9:13]
    gather_pieces(v_ref, own, oth, x_ref)
    first, second = halves(sc_ref)
    sel = sel_ref[:, :]
    lane_pad = jnp.zeros((1, 192), F32)
    for dy in range(4):
        heads, tails = [], []
        for i in range(2):
            e = 2 * dy + i
            at = expert_at(sc_ref, e)
            rows = x_ref[e]
            total = mm(rows[:, :HALF], w_up_ref[at, first, :]) + mm(rows[:, HALF:], w_up_ref[at, second, :])
            parts[dy][i * ESLOT : (i + 1) * ESLOT, :] = total.astype(BF)
            logit = mm_nt(sel, rows)[e : e + 1, :]
            heads.append(logit[:, :256])
            tails.append(jnp.concatenate([logit[:, 256:], lane_pad], axis=1))
        logits = jnp.concatenate(heads + tails, axis=0)
        high = logits.astype(BF).astype(F32)
        low = logits - high
        parts[dy][OWN:, :] = jnp.concatenate([high, low, jnp.zeros((8, 256), F32)], axis=0).astype(BF)


def down_grad_body(sc_ref, v_ref, w_down_ref, *refs):
    own, oth, x_ref, parts = refs[0:4], refs[4:-5], refs[-5], refs[-4:]
    gather_pieces(v_ref, own, oth, x_ref)
    first, second = halves(sc_ref)
    for e in range(NE):
        at = expert_at(sc_ref, e)
        rows = x_ref[e]
        total = mm_nt(rows[:, :HALF], w_down_ref[at, :, first]) + mm_nt(rows[:, HALF:], w_down_ref[at, :, second])
        parts[e // 2][(e % 2) * ESLOT : (e % 2 + 1) * ESLOT, :] = total.astype(BF)


def as_columns(rows):
    turned = jnp.concatenate([rows, jnp.zeros((TOK - rows.shape[0], 256), F32)], axis=0).T
    return jnp.concatenate([turned[:, 0:1], turned[:64, 2:3], turned[:, 1:2], turned[:64, 3:4]], axis=0)


def as_rows(column):
    wide = jnp.broadcast_to(column, (OWN, TOK))
    lane = lax.broadcasted_iota(jnp.int32, (256, TOK), 1)
    pad = jnp.zeros((192, TOK), F32)
    pieces = (
        wide[0:256],
        wide[ESLOT : ESLOT + 256],
        jnp.concatenate([wide[256:ESLOT], pad], axis=0),
        jnp.concatenate([wide[ESLOT + 256 :], pad], axis=0),
    )
    mixed = jnp.zeros((256, TOK), F32)
    for i, piece in enumerate(pieces):
        mixed = jnp.where(lane == i, piece, mixed)
    return mixed.T[:EXT]


def settle_body(p0, p1, p2, p3, hid_ref, pre_ref, gate_ref):
    def total(lo, hi):
        return sum(p[lo:hi, :].astype(F32) for p in (p0, p1, p2, p3))

    extra = total(OWN, OWN + EXT)
    gate = jax.nn.sigmoid(as_columns(extra[0:4] + extra[4:8]))
    pre = total(0, OWN)
    pre_ref[:, :] = pre
    gate_ref[:, :] = jnp.broadcast_to(gate, (OWN, TOK))
    inner = GELU_C * (pre + GELU_A * pre * pre * pre)
    hid_ref[:, :] = (gate * (0.5 * pre * (1.0 + jnp.tanh(inner)))).astype(BF)


def settle_grad_body(*refs):
    parts, (pre_ref, gate_ref, grad_ref) = refs[:-3], refs[-3:]
    total = sum(p[:, :].astype(F32) for p in parts)
    pre = pre_ref[:, :]
    gate = gate_ref[:, 0:1]
    tangent = jnp.tanh(GELU_C * (pre + GELU_A * pre * pre * pre))
    hidden = (0.5 * pre * (1.0 + tangent)).astype(BF).astype(F32)
    slope = 0.5 * (1.0 + tangent) + 0.5 * pre * (1.0 - tangent * tangent) * GELU_C * (1.0 + 3.0 * GELU_A * pre * pre)
    score = jnp.sum(hidden * total, axis=1, keepdims=True)
    grad_ref[0:OWN, :] = (gate * total * slope).astype(BF)
    grad_ref[OWN:, :] = as_rows(score * gate * (1.0 - gate)).astype(BF)


def place_rows(out_ref, e, pair):
    for q in range(QUADS):
        span = slice(q * QCAP, (q + 1) * QCAP)
        out_ref[q, e * QCAP : (e + 2) * QCAP, :] = jnp.concatenate([pair[0][span], pair[1][span]], axis=0).astype(BF)


def scatter_rows(far, put_ref, out_ref, y_ref):
    for q in range(QUADS):
        rows = mm(put_ref[q], out_ref[q]).astype(BF)
        g, i = q // 2, q % 2
        for k in range(2):
            at = ((2 * i + k) * 4 + g if far else 2 * q + k) * 256
            y_ref[at : at + 256, :] = rows[k * 256 : (k + 1) * 256]


def down_body(far, sc_ref, put_ref, w_down_ref, h0, h1, h2, h3, y_ref, out_ref):
    hid = (h0, h1, h2, h3)
    cols = halves(sc_ref)[int(far)]
    for d in range(4):
        pair = [
            mm(hid[d][i * ESLOT : (i + 1) * ESLOT, :], w_down_ref[expert_at(sc_ref, 2 * d + i), :, cols])
            for i in range(2)
        ]
        place_rows(out_ref, 2 * d, pair)
    scatter_rows(far, put_ref, out_ref, y_ref)


def logit_rows(extras):
    rows = []
    for extra in extras:
        extra = extra.astype(F32)
        for i in range(2):
            rows.append(jnp.concatenate([extra[i : i + 1, :], extra[2 + i : 3 + i, :64]], axis=1))
    return jnp.concatenate(rows, axis=0)


def up_grad_body(far, sc_ref, sel_ref, put_ref, w_up_ref, h0, h1, h2, h3, y_ref, out_ref):
    grads = (h0, h1, h2, h3)
    part = slice(HALF, 2 * HALF) if far else slice(0, HALF)
    cols = halves(sc_ref)[int(far)]
    sel = sel_ref[:, part].astype(F32)
    rows = logit_rows([g[OWN:, :] for g in grads])
    rows = jnp.concatenate([rows, jnp.zeros((NE, 64), F32)], axis=1)
    columns = jnp.concatenate([rows, jnp.zeros((TOK - NE, 384), F32)], axis=0).T
    for d in range(4):
        pair = []
        for i in range(2):
            e = 2 * d + i
            out = mm_nt(grads[d][i * ESLOT : (i + 1) * ESLOT, :], w_up_ref[expert_at(sc_ref, e), cols, :])
            pair.append(out + columns[:ESLOT, e : e + 1] * sel[e : e + 1, :])
        place_rows(out_ref, 2 * d, pair)
    scatter_rows(far, put_ref, out_ref, y_ref)


def d_down_body(sc_ref, c0_ref, c1_ref, *refs):
    hid, d_ref = (refs[0:4], refs[4:8]), refs[8]
    first, second = halves(sc_ref)
    for e in range(NE):
        at = expert_at(sc_ref, e)
        span = slice((e % 2) * ESLOT, (e % 2 + 1) * ESLOT)
        for h, cols in enumerate((first, second)):
            part = slice(h * HALF, (h + 1) * HALF)
            d_ref[at, :, cols] = mm_tn(hid[0][e // 2][span, :], c0_ref[e, :, part]) + mm_tn(
                hid[1][e // 2][span, :], c1_ref[e, :, part]
            )


def d_up_body(sc_ref, x0_ref, x1_ref, *refs):
    grads, d_ref = (refs[0:4], refs[4:8]), refs[8]
    first, second = halves(sc_ref)
    for e in range(NE):
        at = expert_at(sc_ref, e)
        span = slice((e % 2) * ESLOT, (e % 2 + 1) * ESLOT)
        for h, cols in enumerate((first, second)):
            part = slice(h * HALF, (h + 1) * HALF)
            d_ref[at, cols, :] = mm_tn(x0_ref[e, :, part], grads[0][e // 2][span, :]) + mm_tn(
                x1_ref[e, :, part], grads[1][e // 2][span, :]
            )


def d_sel_body(sc_ref, x0_ref, x1_ref, *refs):
    grads, code_ref, sel_ref = (refs[0:4], refs[4:8]), refs[8], refs[9]
    first, second = halves(sc_ref)
    rows = [logit_rows([g[OWN:, :] for g in grads[p]]).astype(BF) for p in range(2)]
    for e in range(NE):
        at = expert_at(sc_ref, e)
        d_sel = (mm(rows[0], x0_ref[e]) + mm(rows[1], x1_ref[e]))[e : e + 1, :]
        sel_ref[pl.ds(at, 1), first] = d_sel[:, :HALF]
        sel_ref[pl.ds(at, 1), second] = d_sel[:, HALF:]
    value = jnp.concatenate([sel_ref[:, :HALF], sel_ref[:, HALF:]], axis=0)
    high = value.astype(BF)
    code_ref[: 2 * NE, :] = high
    code_ref[2 * NE :, :] = (value - high.astype(F32)).astype(BF)


def last_sum_body(sc_ref, cot_ref, state_ref, t0, t1, t2, t3, mine_ref, rest_ref):
    core = sc_ref[1]
    terms = (t0, t1, t2, t3)
    for out_ref, side in ((mine_ref, core), (rest_ref, 1 - core)):
        for k, base_ref in enumerate((cot_ref, state_ref)):
            total = base_ref[pl.ds(pl.multiple_of(side * TOK, TOK), TOK), :].astype(F32)
            for term in terms:
                total = total + term[pl.ds(pl.multiple_of((2 * k + side) * TOK, TOK), TOK), :].astype(F32)
            out_ref[k * TOK : (k + 1) * TOK, :] = total.astype(BF)
    for d in range(4):
        rest_ref[(2 + d) * TOK : (3 + d) * TOK, :] = terms[(4 - d) % 4][4 * TOK :, :]


def last_order_body(sc_ref, mine_ref, own_ref, got_ref, cot_ref, state_ref, d_sel_ref, all_ref):
    core = sc_ref[1]
    first, second = halves(sc_ref)
    for k, out_ref in enumerate((cot_ref, state_ref)):
        out_ref[:, first] = mine_ref[k * TOK : (k + 1) * TOK, :]
        out_ref[:, second] = got_ref[k * TOK : (k + 1) * TOK, :]
    for source, side in ((own_ref, core), (got_ref, 1 - core)):
        for d1 in range(4):
            for d2 in range(4):
                x = lax.rem(sc_ref[2] + jnp.where(side == 0, d1, d2), 4)
                z = lax.rem(sc_ref[3] + jnp.where(side == 0, d2, d1), 4)
                to = pl.ds(pl.multiple_of(((x * 4 + z) * 2 + side) * NE, NE), NE)
                at = 2 * TOK + (d1 * 4 + d2) * 32
                block = source[at : at + 32, :].astype(F32)
                value = block[: 2 * NE] + block[2 * NE :]
                all_ref[to, :HALF] = value[:NE]
                all_ref[to, HALF:] = value[NE:]
    d_sel_ref[:, :] = all_ref[:, :].T


def add_swapped_body(own_ref, got_ref, *refs):
    riders, outs = refs[:-4], refs[-4:]
    for g in range(GROUPS):
        span = slice(g * GTOK, (g + 1) * GTOK)
        outs[g][:GTOK, :] = (own_ref[span, :].astype(F32) + got_ref[span, :].astype(F32)).astype(BF)
        for rider in riders:
            outs[g][GTOK:, :] = rider[:, :]


def add_second_body(count, *refs):
    outs = refs[-4:]
    for k in range(count):
        got = refs[4 * k : 4 * k + 4]
        for i in range(4):
            span = slice(i * 256, (i + 1) * 256)
            outs[i][k * 256 : (k + 1) * 256, :] = sum(r[span, :].astype(F32) for r in got).astype(BF)
    if refs[0].shape[0] > GTOK:
        for d in range(4):
            rider = refs[(4 - d) % 4][GTOK:, :]
            for out in outs:
                out[256 * count + 32 * d : 256 * count + 32 * (d + 1), :] = rider


def total_body(a, b, c, d, out_ref):
    out_ref[:, :] = sum(r[:, :].astype(F32) for r in (a, b, c, d)).astype(BF)


def advance_body(base_ref, t0, t1, t2, t3, out_ref):
    step = base_ref.shape[0] // 4
    for j in range(4):
        total = base_ref[j * step : j * step + 256, :].astype(F32)
        for d, term in enumerate((t0, t1, t2, t3)):
            at = (j - d) % 4 * 256
            total = total + term[at : at + 256, :].astype(F32)
        out_ref[j * 256 : (j + 1) * 256, :] = total.astype(BF)


def in_order(got):
    got = dict(zip(ORDER, tie(*[got[d] for d in ORDER])))
    return [got[d] for d in (1, 2, 3)]


def gather_second(stacked):
    own = {d: hop(stacked, 2, -d) for d in ORDER}
    return [stacked, own[1], own[2], own[3]]


def gather_first(mine):
    got = {d: hop(mine, 1, -d) for d in ORDER}
    return jnp.concatenate([mine, *in_order(got)], axis=0)


def scatter_first(own, oth, *riders):
    rows = GTOK + sum(r.shape[0] for r in riders)
    outs = [shape((rows, HALF), BF)] * 4
    return call(add_swapped_body, outs, (own, swap(oth), *riders), moved=6 << 20)


def scatter_second(second):
    return [second[0], *in_order({d: hop(second[d], 2, d) for d in ORDER})]


def stack_body(a, b, c, d, out_ref):
    for i, piece in enumerate((a, b, c, d)):
        out_ref[i * PIECE : (i + 1) * PIECE, :] = piece[:, :]


def no_work(values):
    return values


def advance(base, got, beside=no_work, values=()):
    total = call(total_body, shape((GTOK, HALF), BF), got, moved=3 << 20)
    total, values = tie(total, values)
    terms = [total, *in_order({d: hop(total, 1, -d) for d in ORDER})]
    terms, values = tie(terms, beside(values))
    return call(advance_body, shape((GTOK, HALF), BF), (base, *terms), moved=3 << 20), values


def add_second(*sums):
    rows = 2 * TOK * len(sums) + (128 if sums[0][0].shape[0] > GTOK else 0)
    body = functools.partial(add_second_body, len(sums))
    return call(body, [shape((rows, HALF), BF)] * 4, sum(sums, []), moved=3 << 20)


def scatter_third(first):
    return [first[0], *in_order({d: hop(first[d], 1, d) for d in ORDER})]


def all_dp(block):
    return [block, *in_order({d: hop_dp(block, -d) for d in ORDER})]


def to_dp(parts):
    return [parts[0], *in_order({d: hop_dp(parts[d], d) for d in ORDER})]


def per_device(tokens, picks, halting, w_sel, w_up, w_down, cotangent):
    dp = lax.axis_index("dp")
    place = lax.axis_index("expert")
    core = lax.rem(place, 2)
    sc = jnp.stack([dp, core, place // 8, lax.rem(place // 2, 4)]).astype(jnp.int32)
    rel = lax.rem(2 * dp + jnp.arange(NE, dtype=jnp.int32), NE) + NE * place
    eid = jnp.broadcast_to(rel.astype(F32)[:, None], (NE, 256))
    sel = w_sel.T[rel]
    sel = jnp.where(core == 0, sel, jnp.concatenate([sel[:, HALF:], sel[:, :HALF]], axis=1))

    def mine_of(array):
        return jnp.where(core == 0, array[:, :HALF], array[:, HALF:])

    def rest_of(array):
        return jnp.where(core == 0, array[:, HALF:], array[:, :HALF])

    def by_core(mine, rest):
        return jnp.where(core == 0, jnp.concatenate([mine, rest], axis=0), jnp.concatenate([rest, mine], axis=0))

    live = halting[None, :, None] > jnp.arange(2, dtype=jnp.int32)[:, None, None]
    named = jnp.where(live, picks, EXPERTS).transpose(2, 0, 1).reshape(16, 256).astype(BF)
    rest = swap(jnp.concatenate([rest_of(tokens), named], axis=0))
    state = by_core(mine_of(tokens), rest[:TOK])
    stacked = jnp.concatenate([state, by_core(named, rest[TOK:])], axis=0)
    stacked = [stacked, *in_order({d: hop(stacked, 1, -d) for d in ORDER})]
    stacked = call(stack_body, shape((4 * PIECE, HALF), BF), stacked)
    stacked, cotangent = tie(stacked, cotangent)
    own = gather_second(stacked)
    cot = by_core(mine_of(cotangent), swap(rest_of(cotangent)))
    cot_stacked = gather_first(cot)
    own[2], cot_stacked = tie(own[2], cot_stacked)
    oth = [swap(q) for q in own]
    v = call(
        routing_body,
        shape((2, GROUPS, NE, GTOK), F32),
        (eid, *own),
        moved=1 << 20,
    )

    rows_type = shape((NE, ESLOT, 2 * HALF), BF)
    gather_flops = 2 * 640 * 1024 * 512 * 4 + 2 * 2560 * 512 * 256

    def project_up(v, own, oth):
        return call(
            up_body,
            [rows_type] + [shape((OWN + EXT, HID), BF)] * 4,
            (sc, v, sel, w_up, *own, *oth),
            flops=gather_flops,
            moved=12 << 20,
            smem=1,
        )

    def project_cot(v, own, oth):
        return call(
            down_grad_body,
            [rows_type] + [shape((OWN, HID), BF)] * 4,
            (sc, v, w_down, *own, *oth),
            flops=gather_flops,
            moved=12 << 20,
            smem=1,
        )

    def settle(parts):
        outs = [shape((OWN, HID), BF), shape((OWN, HID), F32), shape((OWN, TOK), F32)]
        return call(settle_body, outs, parts, moved=3 << 20)

    def settle_grad(parts, pre, gate):
        return call(settle_grad_body, shape((OWN + EXT, HID), BF), (*parts, pre, gate), moved=3 << 20)

    def put_of(v):
        return call(put_body, shape((QUADS, QTOK, QSLOT), BF), (v,), flops=4096 * 384 * 256, moved=4 << 20)

    y_type = shape((GROUPS * GTOK, HALF), BF)
    out_scratch = [pltpu.VMEM((QUADS, QSLOT, HALF), BF)]

    def both(body, ins, last):
        def half(far, last):
            return call(
                functools.partial(body, far),
                y_type,
                (*ins, *last),
                flops=gather_flops // 2,
                moved=8 << 20,
                scratch=out_scratch,
                smem=1,
            )

        far = half(True, last)
        far, last = tie(far, last)
        return half(False, last), far

    def outputs(put, hid):
        return both(down_body, (sc, put, w_down), hid)

    def grads_in(put, grads):
        return both(up_grad_body, (sc, sel, put, w_up), grads)

    x0, *parts = project_up(v[0], own, oth)
    parts, cot_stacked = tie(parts, cot_stacked)
    parts = to_dp(parts)
    cot_own = gather_second(cot_stacked)
    parts, cot_own = tie(parts, cot_own)
    hid0, pre0, gate0 = settle(parts)
    put0, put1 = put_of(v[0]), put_of(v[1])
    hid0, cot_own = tie(hid0, cot_own)
    hid0 = all_dp(hid0)
    cot_far = swap(jnp.concatenate(cot_own, axis=0))
    hid0, put0, put1, cot_own, cot_far = tie(hid0, put0, put1, cot_own, cot_far)
    near, far = outputs(put0, hid0)
    near, cot_own, cot_far = tie(near, cot_own, cot_far)
    c1, *cot_parts = project_cot(v[1], cot_own, [cot_far])
    near, cot_parts = tie(near, cot_parts)
    second, cot_parts = tie(scatter_first(near, far), cot_parts)
    got = scatter_second(second)
    cot_parts[2] = hop_dp(cot_parts[2], 2)
    got, cot_parts[2] = tie(got, cot_parts[2])
    state1, (cot_parts[1], cot_parts[3]) = advance(
        stacked, got, lambda two: (hop_dp(two[0], 1), hop_dp(two[1], 3)), (cot_parts[1], cot_parts[3])
    )

    own = gather_second(state1)
    x1, *parts = project_up(v[1], own, [swap(q) for q in own])
    hid1, pre1, gate1 = settle(to_dp(parts))
    grad1 = all_dp(settle_grad(cot_parts, pre1, gate1))

    hid1, grad1 = tie(hid1, grad1)
    second = scatter_first(*grads_in(put1, grad1))
    second, hid1 = tie(second, hid1)
    got = scatter_second(second)
    hid1 = {0: hid1, 2: hop_dp(hid1, -2)}
    got, hid1 = tie(got, hid1)
    cot1, hid1 = advance(
        cot_stacked, got, lambda hid: {**hid, 1: hop_dp(hid[0], -1), 3: hop_dp(hid[0], -3)}, hid1
    )
    hid1 = [hid1[d] for d in range(4)]
    own = gather_second(cot1)
    own[3], hid1 = tie(own[3], hid1)
    out1 = outputs(put1, hid1)
    own[2], out1 = tie(own[2], out1)

    c0, *cot_parts = project_cot(v[0], own, [swap(q) for q in own])
    cot_parts, second = tie(cot_parts, scatter_first(*out1))
    cot_parts = to_dp(cot_parts)
    state_got = {0: second[0], 2: hop(second[2], 2, 2)}
    cot_parts, state_got = tie(cot_parts, state_got)
    grad0 = settle_grad(cot_parts, pre0, gate0)
    grad0, near1, far1, c0 = tie(grad0, second[1], second[3], c0)
    grad0 = all_dp(grad0)
    state_got[1], state_got[3] = hop(near1, 2, 1), hop(far1, 2, 3)
    state_got = [state_got[d] for d in range(4)]
    d_down = call(
        d_down_body,
        shape(w_down.shape, F32),
        (sc, c0, c1, *hid0, *hid1),
        flops=4 * 2560 * 512 * 256,
        moved=16 << 20,
        smem=1,
    )
    grad0, d_down, state_got = tie(grad0, d_down, state_got)
    near, far = grads_in(put0, grad0)
    d_sel = call(
        d_sel_body,
        shape((4 * NE, HALF), BF),
        (sc, x0, x1, *grad0, *grad1),
        moved=8 << 20,
        scratch=[pltpu.VMEM((NE, 2 * HALF), F32)],
        smem=1,
    )
    second = scatter_first(near, far, d_sel)
    second, state_got, grad0 = tie(second, state_got, grad0)
    got = scatter_second(second)
    d_up = call(
        d_up_body,
        shape(w_up.shape, F32),
        (sc, x0, x1, *grad0, *grad1),
        flops=4 * 2560 * 512 * 256,
        moved=16 << 20,
        smem=1,
    )
    got, d_up = tie(got, d_up)
    terms = scatter_third(add_second(got, state_got))
    mine, rest = call(
        last_sum_body,
        [shape((2 * TOK, HALF), BF), shape((6 * TOK, HALF), BF)],
        (sc, cot1, state1, *terms),
        smem=1,
    )
    d_tokens, layer_out, d_sel = call(
        last_order_body,
        [shape((TOK, 2 * HALF), BF)] * 2 + [shape((2 * HALF, EXPERTS), F32)],
        (sc, mine, rest, swap(rest)),
        scratch=[pltpu.VMEM((EXPERTS, 2 * HALF), F32)],
        smem=1,
    )
    return (layer_out, d_tokens, d_up, d_down, d_sel)


def solution(mesh):
    in_specs = (
        P("expert", "dp"),
        P(None, "expert", None),
        P("expert"),
        P("dp", None),
        P("expert", "dp", None),
        P("expert", None, "dp"),
        P("expert", "dp"),
    )
    out_specs = (
        P("expert", "dp"),
        P("expert", "dp"),
        P("expert", "dp", None),
        P("expert", None, "dp"),
        P("dp", None),
    )
    return jax.shard_map(
        per_device, mesh=mesh, in_specs=in_specs, out_specs=out_specs, check_vma=False
    )
```
